128 devices in a mesh: blk: 16 (over z, y), owner: 8 (over x, core).
Axes of the slice: x: 4, y: 4, z: 4, core: 2. Of those that a mesh axis runs over, the one named last changes fastest.
Arguments:
- small_emb: bfloat16 [16384, 4096], P(('blk', 'owner'))
- cluster_of: int32 [16384], P(('blk', 'owner')), may hold values from 0 to 2047, as said below
- big_emb: bfloat16 [32768, 4096], P(('blk', 'owner'))
Outputs:
- small_max: float32 [16384], P(('blk', 'owner'))
- big_max: float32 [32768], P(('blk', 'owner'))
The draws below stay inside these ranges and needn't reach their ends.
Inputs may be any that keep to these rules, and one draw needn't show every extreme that they name: `cluster_of`: cluster c is owned by device c // 16 of the joined axes blk+owner. At most 2 documents of one device lie in the clusters of one owner; in every draw one owner receives exactly 2 documents from every device.
All inputs are finite; a program needn't handle non-finite values.
Results may differ from the reference program's by a relative error of at most 0.00045.
Values may be sent and summed in bfloat16 or wider, within the bound.
A program may use at most 128 MiB of HBM per device.

```python
import math
import jax
import jax.numpy as jnp
from jax import lax

D = 4096
ROW_DEV = 128
BIG_DEV = 256
CPO = 16
CAP = 2
ROWS = 16384
CLUSTERS = 2048
BIG_ROWS = 32768
N_BLK = 16
N_OWNER = 8


def cluster_plan(key):
    devices = N_BLK * N_OWNER
    slots = devices * CAP
    forced = jax.random.randint(jax.random.fold_in(key, 101), (), 0, devices)
    slot_ids = jnp.arange(slots, dtype=jnp.int32)

    def one_source(source):
        source_key = jax.random.fold_in(jax.random.fold_in(key, 102), source)
        shuffled = jax.random.permutation(source_key, slots).astype(jnp.int32)
        scores = jnp.where(slot_ids // CAP == forced, slot_ids % CAP - CAP, shuffled)
        ordering = jnp.argsort(scores, stable=True).astype(jnp.int32)
        taken = ordering[:ROW_DEV]
        mixing = jax.random.permutation(jax.random.fold_in(source_key, 7), ROW_DEV)
        return taken[mixing]
    picked = jax.vmap(one_source)(jnp.arange(devices, dtype=jnp.int32))
    target_owner = picked // CAP
    local_cluster = jax.random.randint(jax.random.fold_in(key, 103), (devices, ROW_DEV), 0, CPO)
    return (target_owner * CPO + local_cluster).reshape(-1).astype(jnp.int32)


def draw_cluster_of(key, part):
    return cluster_plan(key)


def mixed_rows(key, centers, count, low_scale, high_scale):
    noise_key, mix_key, scale_key = jax.random.split(key, 3)
    noise = jax.random.normal(noise_key, (count, D), jnp.float32)
    row_scale = jnp.exp(jax.random.uniform(scale_key, (count, 1), jnp.float32, math.log(low_scale), math.log(high_scale)))
    mixing = jnp.exp(jax.random.uniform(mix_key, (count, 1), jnp.float32, math.log(0.4), math.log(2.0)))
    return row_scale * (centers + mixing * noise)


def draw_small_emb(key, part):
    labels = cluster_plan(key)
    key = jax.random.fold_in(key, 11)
    center_key, row_key = jax.random.split(key)
    centers = jax.random.normal(center_key, (CLUSTERS, D), jnp.float32)
    return mixed_rows(row_key, centers[labels], ROWS, 0.5, 5.0).astype(jnp.bfloat16)


def field_rows(key, count):
    return jax.random.normal(key, (count, D), jnp.float32)


def draw_big_emb(key, part):
    key = jax.random.fold_in(key, 13)
    sub_key, center_key, subc_key, own_key, mix_key, scale_key = jax.random.split(key, 6)
    members = N_BLK * BIG_DEV
    subs = max(members // 64, 1)
    rows = jnp.arange(BIG_ROWS, dtype=jnp.int32)
    group = (rows // BIG_DEV % N_OWNER).astype(jnp.int32)
    sub_id = jax.random.randint(sub_key, (BIG_ROWS,), 0, subs).astype(jnp.int32) + group * subs
    centers = field_rows(center_key, N_OWNER)
    sub_centers = field_rows(subc_key, N_OWNER * subs)
    own_noise = field_rows(own_key, BIG_ROWS)
    sub_mix = jnp.exp(jax.random.uniform(mix_key, (N_OWNER * subs, 1), jnp.float32, math.log(0.7), math.log(1.4)))
    row_scale = jnp.exp(jax.random.uniform(scale_key, (BIG_ROWS, 1), jnp.float32, math.log(0.5), math.log(5.0)))
    vectors = 0.5 * centers[group] + sub_centers[sub_id] + sub_mix[sub_id] * own_noise
    return (row_scale * vectors).astype(jnp.bfloat16)


def setup_inputs(seed: int = 0) -> dict:
    arg_keys = jax.random.split(jax.random.key(seed), 4)
    return {
        "small_emb": draw_small_emb(jax.random.fold_in(arg_keys[3], 71), 0),
        "cluster_of": draw_cluster_of(jax.random.fold_in(arg_keys[3], 71), 0),
        "big_emb": draw_big_emb(jax.random.fold_in(arg_keys[3], 71), 0),
    }


def unit_rows(matrix):
    values = matrix.astype(jnp.float32)
    inverse = lax.rsqrt(lax.optimization_barrier(jnp.sum(values * values, axis=-1, keepdims=True)) + 1e-06)
    return (values * inverse).astype(jnp.bfloat16)

def reference(small_emb, cluster_of, big_emb):
    devices = N_BLK * N_OWNER
    width = devices * CAP
    small_units = unit_rows(small_emb).astype(jnp.float32)
    owner_index = (cluster_of // CPO).astype(jnp.int32)
    ordering = jnp.argsort(owner_index, stable=True).astype(jnp.int32)
    owner_ids = jnp.arange(devices, dtype=jnp.int32)
    counts = lax.optimization_barrier(jnp.sum((owner_index[None, :] == owner_ids[:, None]).astype(jnp.int32), axis=1)).astype(jnp.int32)
    offsets = (jnp.cumsum(counts) - counts).astype(jnp.int32)
    padded_order = jnp.concatenate([ordering, jnp.zeros((width,), jnp.int32)])
    position = jnp.arange(width, dtype=jnp.int32)

    def per_owner(index):
        picked = lax.dynamic_slice(padded_order, (offsets[index],), (width,))
        valid = position < counts[index]
        chosen = small_units[picked]
        labels = jnp.where(valid, cluster_of[picked], -1)
        gram = jnp.dot(chosen, chosen.T, precision=lax.Precision.HIGHEST, preferred_element_type=jnp.float32)
        keep = (labels[:, None] == labels[None, :]) & (position[:, None] != position[None, :]) & valid[None, :]
        highest = lax.optimization_barrier(jnp.max(jnp.where(keep, gram, jnp.float32(-1.0)), axis=1))
        return (highest, jnp.where(valid, picked, ROWS).astype(jnp.int32))
    highest, target = lax.map(per_owner, owner_ids)
    small_max = jnp.full((ROWS + 1,), -1.0, jnp.float32).at[target.reshape(-1)].set(highest.reshape(-1))[:ROWS]
    big_units = unit_rows(big_emb).astype(jnp.float32)
    grouped = big_units.reshape(N_BLK, N_OWNER, BIG_DEV, D).transpose(1, 0, 2, 3).reshape(N_OWNER, N_BLK * BIG_DEV, D)
    group_ids = jnp.arange(N_BLK * BIG_DEV, dtype=jnp.int32)

    def per_group(members):
        gram = jnp.dot(members, members.T, precision=lax.Precision.HIGHEST, preferred_element_type=jnp.float32)
        keep = group_ids[:, None] != group_ids[None, :]
        return lax.optimization_barrier(jnp.max(jnp.where(keep, gram, jnp.float32(-1.0)), axis=1))
    group_max = lax.map(per_group, grouped)
    big_max = group_max.reshape(N_OWNER, N_BLK, BIG_DEV).transpose(1, 0, 2).reshape(-1)
    return (small_max, big_max)
```

```python
import functools

import jax
import jax.numpy as jnp
from jax import lax
from jax.experimental import pallas as pl
from jax.experimental.pallas import tpu as pltpu
from jax.sharding import PartitionSpec as P

MESH = pl.DeviceIdType.MESH
F32 = jnp.float32
BF16 = jnp.bfloat16
CPO = 16
LANES = 128
CHUNK = 32
NC = 8
KC = 1024

HOMES = ((0, 0), (0, -1), (0, -2), (2, -2), (-1, 0), (1, 0), (1, 1), (1, 2))
E0, E1, E2, E3, O1, O2, O3, O4 = range(8)
EARLY_PAIRS = ((E1, E0), (O1, E0), (O2, E0), (O2, E1), (O1, E1), (O2, O1), (O3, O1), (O3, O2))
SMALL_HOPS = [(dy, dz) for dy in range(4) for dz in range(4) if (dy, dz) != (0, 0)]
NEAR_FIRST = (
    (1, 0), (0, 1), (3, 0), (0, 3), (1, 1), (3, 3), (1, 3), (3, 1),
    (2, 2), (2, 0), (0, 2), (2, 1), (1, 2), (2, 3), (3, 2),
)
X_HOPS = ((0, 1), (1, 0), (3, 1), (1, 1), (3, 0), (2, 0), (2, 1))


def pick(index, table):
    value = jnp.int32(table[0])
    for place, entry in enumerate(table[1:], 1):
        value = jnp.where(index == place, jnp.int32(entry), value)
    return value


def nt_dot(a, b):
    return lax.dot_general(a, b, (((1,), (1,)), ((), ())), preferred_element_type=F32)


def unit(values):
    values = values.astype(F32)
    inverse = lax.rsqrt(jnp.sum(values * values, axis=-1, keepdims=True) + 1e-06)
    return (values * inverse).astype(BF16)


def fold(values):
    rows, cols = values.shape
    return jnp.max(values.reshape(rows // 8, 8, cols), axis=0)


def iota(shape, dim):
    return lax.broadcasted_iota(jnp.int32, shape, dim)


def kernel(
    small_ref, cluster_ref, big_ref, small_out, big_out,
    hold, units, sbuf, rbuf, qbuf, tbuf, acc, rowacc, colacc, vsend, vbuf, wsend, wbuf, retsend, ret,
    big_ssem, big_rsem, yz_ssem, yz_rsem, x_ssem, x_rsem, v_ssem, v_rsem, w_ssem, w_rsem, ret_ssem, ret_rsem,
):
    width = small_ref.shape[1]
    wide = width + LANES
    rows = small_ref.shape[0]
    slots = 2 * rows
    b = lax.axis_index("blk")
    o = lax.axis_index("owner")
    z, y = b // 4, b % 4
    x, core = o // 2, o % 2
    sign = 1 - 2 * core
    hub = (y + core) % 2 == 0

    def blk_at(dy, dz):
        return (z + dz + 4) % 4 * 4 + (y + dy + 4) % 4

    def turned(dy, dz):
        return {"blk": blk_at(sign * dy, dz), "owner": o}

    def row_at(dx, dc):
        return (x + dx) % 4 * 2 + (core + dc) % 2

    barrier = pltpu.get_barrier_semaphore()
    for dy, dz in SMALL_HOPS:
        pl.semaphore_signal(barrier, inc=1, device_id={"blk": blk_at(dy, dz), "owner": o}, device_id_type=MESH)
    for dx, dc in X_HOPS:
        pl.semaphore_signal(barrier, inc=1, device_id={"blk": b, "owner": row_at(dx, dc)}, device_id_type=MESH)

    cluster_lanes = jnp.broadcast_to(cluster_ref[...], (rows, rows))
    cluster_rows = jnp.transpose(cluster_lanes.astype(F32)).astype(jnp.int32)
    owner_lanes, owner_rows = cluster_lanes // CPO, cluster_rows // CPO
    earlier = (owner_lanes == owner_rows) & (iota((rows, rows), 0) < iota((rows, rows), 1))
    rank = jnp.sum(jnp.where(earlier, 1.0, 0.0), axis=0, keepdims=True).astype(jnp.int32)
    owner_of_doc = cluster_ref[...] // CPO
    slot_of_doc = owner_of_doc * 2 + rank
    place = jnp.where(iota((slots, rows), 0) == slot_of_doc, 1.0, 0.0).astype(BF16)
    label = jnp.where(iota((rows, LANES), 1) == cluster_rows % CPO, 1.0, 0.0).astype(BF16)

    @pl.loop(0, rows // 16)
    def _(step):
        at = pl.ds(pl.multiple_of(step * 16, 16), 16)
        units[at, :] = unit(small_ref[at, :])

    @pl.loop(0, width // 512)
    def _(step):
        at = pl.ds(pl.multiple_of(step * 512, 512), 512)
        sbuf[:, at] = jnp.dot(place, units[:, at], preferred_element_type=F32).astype(BF16)

    sbuf[:, pl.ds(width, LANES)] = jnp.dot(place, label, preferred_element_type=F32).astype(BF16)

    pl.semaphore_wait(barrier, len(SMALL_HOPS) + len(X_HOPS))

    def yz_copy(n):
        dy, dz = NEAR_FIRST[n]
        to = blk_at(dy, dz)
        return pltpu.make_async_remote_copy(
            src_ref=sbuf.at[pl.ds(pl.multiple_of(to * 16, 16), 16)],
            dst_ref=rbuf.at[pl.ds(pl.multiple_of(b * 16, 16), 16)],
            send_sem=yz_ssem.at[n],
            recv_sem=yz_rsem.at[n],
            device_id={"blk": to, "owner": o},
            device_id_type=MESH,
        )

    for n in range(15):
        yz_copy(n).start()
    mine = pl.ds(pl.multiple_of(b * 16, 16), 16)
    rbuf[mine, :] = sbuf[mine, :]

    def big_copy(lane, c, slot, to_slot, to):
        at = pl.ds(pl.multiple_of(c * CHUNK, CHUNK), CHUNK)
        return pltpu.make_async_remote_copy(
            src_ref=hold.at[slot, at],
            dst_ref=hold.at[to_slot, at],
            send_sem=big_ssem.at[lane, c],
            recv_sem=big_rsem.at[to_slot, c],
            device_id=turned(*to),
            device_id_type=MESH,
        )

    def own_right(c):
        return big_copy(0, c, E0, E1, (0, 1))

    def e1_right(c):
        return big_copy(1, c, E1, E2, (0, 1))

    def e2_down(c):
        return big_copy(2, c, E2, 1, (-1, 0))

    def o2_left(c):
        return big_copy(3, c, O2, O3, (0, -1))

    def o3_left(c):
        return big_copy(4, c, O3, O4, (0, -1))

    def own_up(c):
        return big_copy(0, c, 0, O1, (1, 0))

    def own_down(c):
        return big_copy(1, c, 0, O2, (-1, 0))

    def relay_down(c):
        return big_copy(2, c, 1, E3, (-1, 0))

    def arrived(slot, c):
        big_copy(0, c, slot, slot, (0, 1)).wait_recv()

    @pl.loop(0, NC)
    def _(c):
        for part in range(CHUNK // 16):
            at = pl.ds(pl.multiple_of(c * CHUNK + part * 16, 16), 16)
            hold[0, at, :] = unit(big_ref[at, :])

        @pl.when(hub)
        def _():
            own_right(c).start()

        @pl.when(jnp.logical_not(hub))
        def _():
            own_down(c).start()
            own_up(c).start()

    rowacc[...] = jnp.full(rowacc.shape, -1.0, F32)
    colacc[...] = jnp.full(colacc.shape, -1.0, F32)

    def product(m, left, right):
        acc[pl.ds(0, m), :] = nt_dot(left(0), right(0))

        @pl.loop(1, width // KC)
        def _(k):
            acc[pl.ds(0, m), :] += nt_dot(left(k), right(k))

    def features(k):
        return pl.ds(pl.multiple_of(k * KC, KC), KC)

    def pair(i, r, m, j):
        at = pl.ds(r, m)
        product(m, lambda k: hold[i, at, features(k)], lambda k: hold[j, :, features(k)])
        gram = acc[pl.ds(0, m), :]
        half = gram.shape[1] // 2
        rowacc[i, at, :] = jnp.maximum(rowacc[i, at, :], jnp.maximum(gram[:, :half], gram[:, half:]))
        colacc[j] = jnp.maximum(colacc[j], fold(gram))

    def own_pairs():
        product(hold.shape[1], lambda k: hold[0, :, features(k)], lambda k: hold[0, :, features(k)])
        gram = acc[...]
        gram = jnp.where(iota(gram.shape, 0) == iota(gram.shape, 1), -1.0, gram)
        colacc[0] = jnp.maximum(colacc[0], fold(gram))

    def some_pairs(table, r, m):
        @pl.loop(0, len(table))
        def _(p):
            pair(pick(p, [t[0] for t in table]), r, m, pick(p, [t[1] for t in table]))

    def on(role, body):
        pl.when(hub if role else jnp.logical_not(hub))(body)

    def x_copy(n):
        dx, dc = X_HOPS[n]
        to = row_at(dx, dc)
        return pltpu.make_async_remote_copy(
            src_ref=qbuf.at[pl.ds(pl.multiple_of(to * 32, 32), 32)],
            dst_ref=tbuf.at[pl.ds(pl.multiple_of(o * 32, 32), 32)],
            send_sem=x_ssem.at[n],
            recv_sem=x_rsem.at[n],
            device_id={"blk": b, "owner": to},
            device_id_type=MESH,
        )

    def regroup():
        for n in range(15):
            yz_copy(n).wait_recv()
        to_row = iota((slots, slots), 0)
        source = to_row % 32 // 2 * 16 + to_row // 32 * 2 + to_row % 2
        move = jnp.where(iota((slots, slots), 1) == source, 1.0, 0.0).astype(BF16)

        @pl.loop(0, width // 512)
        def _(step):
            at = pl.ds(pl.multiple_of(step * 512, 512), 512)
            qbuf[:, at] = jnp.dot(move, rbuf[:, at], preferred_element_type=F32).astype(BF16)

        tail = pl.ds(width, LANES)
        qbuf[:, tail] = jnp.dot(move, rbuf[:, tail], preferred_element_type=F32).astype(BF16)
        for n in range(7):
            x_copy(n).start()
        here = pl.ds(pl.multiple_of(o * 32, 32), 32)
        tbuf[here, :] = qbuf[here, :]

    def v_copy(n):
        to = row_at(*X_HOPS[n])
        return pltpu.make_async_remote_copy(
            src_ref=vsend, dst_ref=vbuf.at[o], send_sem=v_ssem.at[n], recv_sem=v_rsem.at[n],
            device_id={"blk": b, "owner": to}, device_id_type=MESH,
        )

    def w_copy(n):
        to = blk_at(*NEAR_FIRST[n])
        return pltpu.make_async_remote_copy(
            src_ref=wsend, dst_ref=wbuf.at[b], send_sem=w_ssem.at[n], recv_sem=w_rsem.at[n],
            device_id={"blk": to, "owner": o}, device_id_type=MESH,
        )

    def owner_maxima():
        for n in range(7):
            x_copy(n).wait_recv()
        product(slots, lambda k: tbuf[:, features(k)], lambda k: tbuf[:, features(k)])
        labels = tbuf[:, pl.ds(width, LANES)]
        same = nt_dot(labels, labels) > 0.5
        same = same & (iota((slots, slots), 0) != iota((slots, slots), 1))
        best = jnp.max(jnp.where(same, acc[...], -1.0), axis=0, keepdims=True)
        vsend[...] = jnp.broadcast_to(best, vsend.shape)
        for n in range(7):
            v_copy(n).start()
        vbuf[o] = vsend[...]

    def pass_back():
        for n in range(7):
            v_copy(n).wait_recv()
        packed = vbuf[0]
        for other in range(1, 8):
            packed = jnp.where(iota(packed.shape, 0) == other, vbuf[other], packed)
        packed = pltpu.roll(packed, (8 - o) * 32 % slots, 1)
        wsend[...] = packed[:, :LANES]
        for n in range(15):
            w_copy(n).start()
        wbuf[b] = wsend[...]

    def small_result():
        for n in range(15):
            w_copy(n).wait_recv()
        table = wbuf[...].reshape(16 * 8, LANES)
        chosen = jnp.where(iota((16 * 8, rows), 0) == owner_of_doc, 1.0, 0.0)
        found = lax.dot_general(
            table, chosen, (((0,), (0,)), ((), ())), precision=lax.Precision.HIGHEST, preferred_element_type=F32
        )
        found = jnp.where(iota(found.shape, 0) == 2 * b + rank, found, 0.0)
        small_out[...] = jnp.sum(found, axis=0, keepdims=True)

    def first_steps(start, stop):
        def body():
            @pl.loop(start, stop)
            def _(c):
                arrived(O2, c)
                o2_left(c).start()

                @pl.when(c >= 5)
                def _():
                    arrived(E1, c - 5)
                    e1_right(c - 5).start()
                    arrived(O3, c - 5)
                    o3_left(c - 5).start()

        return body

    on(True, first_steps(0, 1))
    regroup()
    on(True, first_steps(1, NC))

    def rest_of_first():
        @pl.loop(3, NC)
        def _(c):
            arrived(E1, c)
            e1_right(c).start()
            arrived(O3, c)
            o3_left(c).start()

        @pl.loop(0, NC)
        def _(c):
            arrived(O1, c)

    on(True, rest_of_first)

    def second_steps(start, stop):
        def body():
            @pl.loop(start, stop)
            def _(c):
                arrived(E2, c)
                e2_down(c).start()
                pair(pick(c, [t[0] for t in EARLY_PAIRS]), 0, 256, pick(c, [t[1] for t in EARLY_PAIRS]))

        return body

    def relay_steps(start, stop):
        def body():
            @pl.loop(start, stop)
            def _(c):
                arrived(1, c)
                relay_down(c).start()

        return body

    on(False, relay_steps(0, 4))
    on(True, second_steps(0, 4))
    own_pairs()
    owner_maxima()
    on(False, relay_steps(4, 6))
    on(True, second_steps(4, 6))
    pass_back()
    on(False, relay_steps(6, NC))
    on(True, second_steps(6, NC))

    def half_pairs(start):
        @pl.loop(0, 4)
        def _(c):
            arrived(O4, c + start // CHUNK)

        some_pairs(((E2, E0), (E2, O1), (E2, O2), (E2, O3), (O4, O1), (O4, O2)), start, 128)

    def late_pairs():
        half_pairs(0)
        half_pairs(128)

    on(True, late_pairs)
    small_result()

    def finish(slot):
        whole = jnp.maximum(fold(jnp.transpose(rowacc[slot])), colacc[slot])
        return jnp.broadcast_to(jnp.max(whole, axis=0, keepdims=True), whole.shape)

    def home_copy(slot):
        return pltpu.make_async_remote_copy(
            src_ref=retsend.at[slot], dst_ref=ret.at[slot], send_sem=ret_ssem.at[slot], recv_sem=ret_rsem.at[slot],
            device_id=turned(*HOMES[slot]), device_id_type=MESH,
        )

    def send_home(slots_done):
        for slot in slots_done:
            retsend[slot] = finish(slot)
            home_copy(slot).start()

    def last_pairs():
        send_home((O1, O2, O4))

        @pl.loop(0, 4)
        def _(c):
            arrived(E3, c)

        last = ((E3, E0), (E3, E1), (E3, O3), (E3, E2))
        some_pairs(last, 0, 128)

        @pl.loop(4, NC)
        def _(c):
            arrived(E3, c)

        some_pairs(last, 128, 128)
        send_home((E3, E2, E1, O3))
        retsend[0] = finish(0)
        for slot in (E1, E2, E3):
            home_copy(slot).wait_recv()
            retsend[0] = jnp.maximum(retsend[0], ret[slot])
        big_out[...] = retsend[0][0:1]

        for slot in range(1, 8):
            home_copy(slot).wait_send()

        @pl.loop(0, NC)
        def _(c):
            own_right(c).wait_send()
            e1_right(c).wait_send()
            e2_down(c).wait_send()
            o2_left(c).wait_send()
            o3_left(c).wait_send()

    def last_relay():
        retsend[0] = finish(0)
        for slot in (O1, O2, O3, O4):
            home_copy(slot).wait_recv()
            retsend[0] = jnp.maximum(retsend[0], ret[slot])
        big_out[...] = retsend[0][0:1]

        @pl.loop(0, NC)
        def _(c):
            own_up(c).wait_send()
            own_down(c).wait_send()
            relay_down(c).wait_send()

    on(True, last_pairs)
    on(False, last_relay)
    for n in range(15):
        yz_copy(n).wait_send()
        w_copy(n).wait_send()
    for n in range(7):
        x_copy(n).wait_send()
        v_copy(n).wait_send()


def body(small_emb, cluster_of, big_emb):
    rows, width = small_emb.shape
    count = big_emb.shape[0]
    wide = width + LANES
    dma = pltpu.SemaphoreType.DMA
    small_max, big_max = pl.pallas_call(
        kernel,
        out_shape=(jax.ShapeDtypeStruct((1, rows), F32), jax.ShapeDtypeStruct((1, count), F32)),
        in_specs=[pl.BlockSpec(memory_space=pltpu.VMEM)] * 3,
        out_specs=[pl.BlockSpec(memory_space=pltpu.VMEM)] * 2,
        scratch_shapes=[
            pltpu.VMEM((8, count, width), BF16),
            pltpu.VMEM((rows, width), BF16),
            pltpu.VMEM((2 * rows, wide), BF16),
            pltpu.VMEM((2 * rows, wide), BF16),
            pltpu.VMEM((2 * rows, wide), BF16),
            pltpu.VMEM((2 * rows, wide), BF16),
            pltpu.VMEM((count, count), F32),
            pltpu.VMEM((8, count, count // 2), F32),
            pltpu.VMEM((8, 8, count), F32),
            pltpu.VMEM((8, 2 * rows), F32),
            pltpu.VMEM((8, 8, 2 * rows), F32),
            pltpu.VMEM((8, LANES), F32),
            pltpu.VMEM((16, 8, LANES), F32),
            pltpu.VMEM((8, 8, count), F32),
            pltpu.VMEM((8, 8, count), F32),
            dma((5, NC)), dma((8, NC)), dma((15,)), dma((15,)), dma((7,)), dma((7,)),
            dma((7,)), dma((7,)), dma((15,)), dma((15,)), dma((8,)), dma((8,)),
        ],
        compiler_params=pltpu.CompilerParams(
            collective_id=0, has_side_effects=True, vmem_limit_bytes=56 * 2**20
        ),
    )(small_emb, cluster_of.reshape(1, rows), big_emb)
    return small_max.reshape(rows), big_max.reshape(count)


def solution(mesh):
    return jax.shard_map(
        body,
        mesh=mesh,
        in_specs=(P(("blk", "owner"), None), P(("blk", "owner")), P(("blk", "owner"), None)),
        out_specs=(P(("blk", "owner")), P(("blk", "owner"))),
        check_vma=False,
    )
```

```python
import functools

import jax
import jax.numpy as jnp
from jax import lax
from jax.experimental import pallas as pl
from jax.experimental.pallas import tpu as pltpu
from jax.sharding import PartitionSpec as P

MESH = pl.DeviceIdType.MESH
F32 = jnp.float32
BF16 = jnp.bfloat16
CPO = 16
LANES = 128
CHUNK = 32
NC = 8
KC = 1024

HOMES = ((0, -2), (0, -1), (0, 0), (1, 1), (1, 0), (-1, 0), (1, 2), (2, -2))
E2, E1, E0, O3, O2, O1, O4, E3 = range(8)
GATE = 6
SMALL_HOPS = [(dy, dz) for dy in range(4) for dz in range(4) if (dy, dz) != (0, 0)]
NEAR_FIRST = (
    (1, 0), (0, 1), (3, 0), (0, 3), (1, 1), (3, 3), (1, 3), (3, 1),
    (2, 2), (2, 0), (0, 2), (2, 1), (1, 2), (2, 3), (3, 2),
)
X_HOPS = ((0, 1), (1, 0), (3, 1), (1, 1), (3, 0), (2, 0), (2, 1))


def pick(index, table):
    value = jnp.int32(table[0])
    for place, entry in enumerate(table[1:], 1):
        value = jnp.where(index == place, jnp.int32(entry), value)
    return value


def nt_dot(a, b):
    return lax.dot_general(a, b, (((1,), (1,)), ((), ())), preferred_element_type=F32)


def unit(values):
    values = values.astype(F32)
    inverse = lax.rsqrt(jnp.sum(values * values, axis=-1, keepdims=True) + 1e-06)
    return (values * inverse).astype(BF16)


def fold(values):
    rows, cols = values.shape
    return jnp.max(values.reshape(rows // 8, 8, cols), axis=0)


def iota(shape, dim):
    return lax.broadcasted_iota(jnp.int32, shape, dim)


def kernel(
    small_ref, cluster_ref, big_ref, small_out, big_out,
    hold, units, sbuf, rbuf, qbuf, tbuf, acc, rowacc, colacc, vsend, vbuf, wsend, wbuf, retsend, ret,
    big_ssem, big_rsem, yz_ssem, yz_rsem, x_ssem, x_rsem, v_ssem, v_rsem, w_ssem, w_rsem, ret_ssem, ret_rsem,
):
    width = small_ref.shape[1]
    wide = width + LANES
    rows = small_ref.shape[0]
    slots = 2 * rows
    b = lax.axis_index("blk")
    o = lax.axis_index("owner")
    z, y = b // 4, b % 4
    x, core = o // 2, o % 2
    sign = 1 - 2 * core
    hub = (y + core) % 2 == 0

    def blk_at(dy, dz):
        return (z + dz + 4) % 4 * 4 + (y + dy + 4) % 4

    def turned(dy, dz):
        return {"blk": blk_at(sign * dy, dz), "owner": o}

    def row_at(dx, dc):
        return (x + dx) % 4 * 2 + (core + dc) % 2

    barrier = pltpu.get_barrier_semaphore()
    for dy, dz in SMALL_HOPS:
        pl.semaphore_signal(barrier, inc=1, device_id={"blk": blk_at(dy, dz), "owner": o}, device_id_type=MESH)
    for dx, dc in X_HOPS:
        pl.semaphore_signal(barrier, inc=1, device_id={"blk": b, "owner": row_at(dx, dc)}, device_id_type=MESH)

    cluster_lanes = jnp.broadcast_to(cluster_ref[...], (rows, rows))
    cluster_rows = jnp.transpose(cluster_lanes.astype(F32)).astype(jnp.int32)
    owner_lanes, owner_rows = cluster_lanes // CPO, cluster_rows // CPO
    earlier = (owner_lanes == owner_rows) & (iota((rows, rows), 0) < iota((rows, rows), 1))
    rank = jnp.sum(jnp.where(earlier, 1.0, 0.0), axis=0, keepdims=True).astype(jnp.int32)
    owner_of_doc = cluster_ref[...] // CPO
    slot_of_doc = owner_of_doc % 8 * 32 + owner_of_doc // 8 * 2 + rank
    place = jnp.where(iota((slots, rows), 0) == slot_of_doc, 1.0, 0.0).astype(BF16)
    label = jnp.where(iota((rows, LANES), 1) == cluster_rows % CPO, 1.0, 0.0).astype(BF16)

    @pl.loop(0, rows // 16)
    def _(step):
        at = pl.ds(pl.multiple_of(step * 16, 16), 16)
        units[at, :] = unit(small_ref[at, :])

    @pl.loop(0, width // 512)
    def _(step):
        at = pl.ds(pl.multiple_of(step * 512, 512), 512)
        sbuf[:, at] = jnp.dot(place, units[:, at], preferred_element_type=F32).astype(BF16)

    sbuf[:, pl.ds(width, LANES)] = jnp.dot(place, label, preferred_element_type=F32).astype(BF16)

    pl.semaphore_wait(barrier, len(SMALL_HOPS) + len(X_HOPS))

    def big_copy(lane, c, slot, to_slot, to):
        at = pl.ds(pl.multiple_of(c * CHUNK, CHUNK), CHUNK)
        return pltpu.make_async_remote_copy(
            src_ref=hold.at[slot, at],
            dst_ref=hold.at[to_slot, at],
            send_sem=big_ssem.at[lane, c],
            recv_sem=big_rsem.at[to_slot, c],
            device_id=turned(*to),
            device_id_type=MESH,
        )

    def own_right(c):
        return big_copy(0, c, E0, E1, (0, 1))

    def e1_right(c):
        return big_copy(1, c, E1, E2, (0, 1))

    def e2_down(c):
        return big_copy(2, c, E2, E3, (-2, 0))

    def o2_left(c):
        return big_copy(3, c, O2, O3, (0, -1))

    def o3_left(c):
        return big_copy(4, c, O3, O4, (0, -1))

    def own_up(c):
        return big_copy(0, c, E0, O1, (1, 0))

    def own_down(c):
        return big_copy(1, c, E0, O2, (-1, 0))

    def arrived(slot, c):
        big_copy(0, c, slot, slot, (0, 1)).wait_recv()

    def send_own(c):
        for part in range(CHUNK // 16):
            at = pl.ds(pl.multiple_of(c * CHUNK + part * 16, 16), 16)
            hold[E0, at, :] = unit(big_ref[at, :])

        @pl.when(hub)
        def _():
            own_right(c).start()

        @pl.when(jnp.logical_not(hub))
        def _():
            own_down(c).start()
            own_up(c).start()

    def x_copy(n):
        dx, dc = X_HOPS[n]
        to = row_at(dx, dc)
        return pltpu.make_async_remote_copy(
            src_ref=sbuf.at[pl.ds(pl.multiple_of(to * 32, 32), 32)],
            dst_ref=rbuf.at[pl.ds(pl.multiple_of(o * 32, 32), 32)],
            send_sem=x_ssem.at[n],
            recv_sem=x_rsem.at[n],
            device_id={"blk": b, "owner": to},
            device_id_type=MESH,
        )

    for n in range(7):
        x_copy(n).start()
    mine = pl.ds(pl.multiple_of(o * 32, 32), 32)
    rbuf[mine, :] = sbuf[mine, :]

    pl.loop(0, NC)(send_own)

    rowacc[...] = jnp.full(rowacc.shape, -1.0, F32)
    colacc[...] = jnp.full(colacc.shape, -1.0, F32)

    def product(m, n, left, right):
        at = (pl.ds(0, m), pl.ds(0, n))
        acc[at] = nt_dot(left(0), right(0))

        @pl.loop(1, width // KC)
        def _(k):
            acc[at] += nt_dot(left(k), right(k))

    def features(k):
        return pl.ds(pl.multiple_of(k * KC, KC), KC)

    def meet(first, count, slot, r, n):
        size = hold.shape[1]
        m = count * size
        product(
            m,
            n,
            lambda k: hold[pl.ds(first, count), :, features(k)].reshape(m, KC),
            lambda k: hold[slot, pl.ds(r, n), features(k)],
        )
        for step in range(count):
            gram = acc[pl.ds(step * size, size), pl.ds(0, n)]
            if first + step == slot:
                gram = jnp.where(iota(gram.shape, 0) == iota(gram.shape, 1) + r, -1.0, gram)
            at = pl.ds(r, n)
            colacc[slot, :, at] = jnp.maximum(colacc[slot, :, at], fold(gram))
            if first + step != slot:
                for part in range(n // LANES):
                    here = gram[:, part * LANES : (part + 1) * LANES]
                    rowacc[first + step] = jnp.maximum(rowacc[first + step], here)

    def on(role, body):
        pl.when(hub if role else jnp.logical_not(hub))(body)

    def yz_copy(n):
        dy, dz = NEAR_FIRST[n]
        to = blk_at(dy, dz)
        return pltpu.make_async_remote_copy(
            src_ref=qbuf.at[pl.ds(pl.multiple_of(to * 16, 16), 16)],
            dst_ref=tbuf.at[pl.ds(pl.multiple_of(b * 16, 16), 16)],
            send_sem=yz_ssem.at[n],
            recv_sem=yz_rsem.at[n],
            device_id={"blk": to, "owner": o},
            device_id_type=MESH,
        )

    def regroup():
        for n in range(7):
            x_copy(n).wait_recv()
        to_row = iota((slots, slots), 0)
        source = to_row % 16 // 2 * 32 + to_row // 16 * 2 + to_row % 2
        move = jnp.where(iota((slots, slots), 1) == source, 1.0, 0.0).astype(BF16)

        @pl.loop(0, width // 512)
        def _(step):
            at = pl.ds(pl.multiple_of(step * 512, 512), 512)
            qbuf[:, at] = jnp.dot(move, rbuf[:, at], preferred_element_type=F32).astype(BF16)

        tail = pl.ds(width, LANES)
        qbuf[:, tail] = jnp.dot(move, rbuf[:, tail], preferred_element_type=F32).astype(BF16)
        for n in range(15):
            yz_copy(n).start()
        here = pl.ds(pl.multiple_of(b * 16, 16), 16)
        tbuf[here, :] = qbuf[here, :]

    def v_copy(n):
        to = blk_at(*NEAR_FIRST[n])
        return pltpu.make_async_remote_copy(
            src_ref=vsend, dst_ref=vbuf.at[b], send_sem=v_ssem.at[n], recv_sem=v_rsem.at[n],
            device_id={"blk": to, "owner": o}, device_id_type=MESH,
        )

    def w_copy(n):
        to = row_at(*X_HOPS[n])
        return pltpu.make_async_remote_copy(
            src_ref=wsend, dst_ref=wbuf.at[o], send_sem=w_ssem.at[n], recv_sem=w_rsem.at[n],
            device_id={"blk": b, "owner": to}, device_id_type=MESH,
        )

    def owner_maxima():
        for n in range(15):
            yz_copy(n).wait_recv()
        product(slots, slots, lambda k: tbuf[:, features(k)], lambda k: tbuf[:, features(k)])
        labels = tbuf[:, pl.ds(width, LANES)]
        same = nt_dot(labels, labels) > 0.5
        same = same & (iota((slots, slots), 0) != iota((slots, slots), 1))
        best = jnp.max(jnp.where(same, acc[pl.ds(0, slots), :], -1.0), axis=0, keepdims=True)
        vsend[...] = jnp.broadcast_to(best, vsend.shape)
        for n in range(15):
            v_copy(n).start()
        vbuf[b] = vsend[...]

    def pass_back():
        for n in range(15):
            v_copy(n).wait_recv()
        for group in range(2):
            packed = vbuf[group * 8]
            for other in range(1, 8):
                packed = jnp.where(iota(packed.shape, 0) == other, vbuf[group * 8 + other], packed)
            packed = pltpu.roll(packed, (16 - b) * 16 % slots, 1)
            wsend[pl.ds(group * 8, 8), :] = packed[:, :LANES]
        for n in range(7):
            w_copy(n).start()
        wbuf[o] = wsend[...]

    def small_result():
        for n in range(7):
            w_copy(n).wait_recv()
        table = wbuf[...].reshape(8 * 16, LANES)
        row_of_doc = owner_of_doc % 8 * 16 + owner_of_doc // 8
        chosen = jnp.where(iota((8 * 16, rows), 0) == row_of_doc, 1.0, 0.0)
        found = lax.dot_general(
            table, chosen, (((0,), (0,)), ((), ())), precision=lax.Precision.HIGHEST, preferred_element_type=F32
        )
        found = jnp.where(iota(found.shape, 0) == 2 * o + rank, found, 0.0)
        small_out[...] = jnp.sum(found, axis=0, keepdims=True)

    def first_steps():
        @pl.loop(0, NC)
        def _(c):
            arrived(O2, c)
            o2_left(c).start()

            @pl.when(c >= GATE)
            def _():
                arrived(E1, c - GATE)
                e1_right(c - GATE).start()

        @pl.loop(NC - GATE, NC)
        def _(c):
            arrived(E1, c)
            e1_right(c).start()

        @pl.loop(0, NC)
        def _(c):
            arrived(O3, c)
            o3_left(c).start()

    def second_step(c, then):
        def body():
            arrived(E2, c)
            e2_down(c).start()
            then()

        return body

    def wait_all(slot, start, stop):
        @pl.loop(start, stop)
        def _(c):
            arrived(slot, c)

    def half(slot, part, first, count):
        start = part * NC // 2
        if slot != E2:
            wait_all(slot, start, start + NC // 2)
        meet(first, count, slot, part * 128, 128)

    on(False, lambda: meet(E0, 1, E0, 0, 256))
    on(True, first_steps)
    regroup()
    on(True, lambda: wait_all(O1, 0, NC))
    on(True, second_step(0, lambda: meet(E1, 4, O1, 0, 256)))
    on(True, second_step(1, lambda: meet(E1, 3, O2, 0, 256)))
    on(True, second_step(2, lambda: meet(E1, 2, E0, 0, 256)))
    on(True, second_step(3, lambda: half(E2, 0, E0, 4)))
    on(True, second_step(4, lambda: half(O4, 0, O2, 2)))
    on(True, second_step(5, lambda: None))
    on(True, second_step(6, lambda: half(E3, 0, E1, 3)))
    on(True, second_step(7, lambda: half(E2, 1, E0, 4)))
    on(True, lambda: half(O4, 1, O2, 2))
    owner_maxima()

    def finish(slot):
        whole = jnp.maximum(fold(jnp.transpose(rowacc[slot])), colacc[slot])
        return jnp.broadcast_to(jnp.max(whole, axis=0, keepdims=True), whole.shape)

    def home_copy(slot):
        return pltpu.make_async_remote_copy(
            src_ref=retsend.at[slot], dst_ref=ret.at[slot], send_sem=ret_ssem.at[slot], recv_sem=ret_rsem.at[slot],
            device_id=turned(*HOMES[slot]), device_id_type=MESH,
        )

    def send_home(slots_done):
        for slot in slots_done:
            retsend[slot] = finish(slot)
            home_copy(slot).start()

    def big_result(others):
        best = finish(E0)
        for slot in others:
            home_copy(slot).wait_recv()
            best = jnp.maximum(best, ret[slot])
        big_out[...] = best[0:1]

    def last_pairs():
        send_home((O1, O2, O4))
        half(E3, 1, E2, 4)
        meet(E2, 1, E3, 0, 128)
        send_home((E3, E2, E1, O3))

    def end_hub():
        big_result((E1, E2, E3))

        for slot in (E1, E2, E3, O1, O2, O3, O4):
            home_copy(slot).wait_send()

        @pl.loop(0, NC)
        def _(c):
            own_right(c).wait_send()
            e1_right(c).wait_send()
            e2_down(c).wait_send()
            o2_left(c).wait_send()
            o3_left(c).wait_send()

    def last_relay():
        big_result((O1, O2, O3, O4))

        @pl.loop(0, NC)
        def _(c):
            own_up(c).wait_send()
            own_down(c).wait_send()

    on(True, last_pairs)
    pass_back()
    small_result()
    on(True, end_hub)
    on(False, last_relay)
    for n in range(15):
        yz_copy(n).wait_send()
        v_copy(n).wait_send()
    for n in range(7):
        x_copy(n).wait_send()
        w_copy(n).wait_send()


def body(small_emb, cluster_of, big_emb):
    rows, width = small_emb.shape
    count = big_emb.shape[0]
    wide = width + LANES
    dma = pltpu.SemaphoreType.DMA
    small_max, big_max = pl.pallas_call(
        kernel,
        out_shape=(pltpu.VMEM((1, rows), F32), pltpu.VMEM((1, count), F32)),
        in_specs=[pl.BlockSpec(memory_space=pltpu.VMEM)] * 3,
        out_specs=[pl.BlockSpec(memory_space=pltpu.VMEM)] * 2,
        scratch_shapes=[
            pltpu.VMEM((8, count, width), BF16),
            pltpu.VMEM((rows, width), BF16),
            pltpu.VMEM((2 * rows, wide), BF16),
            pltpu.VMEM((2 * rows, wide), BF16),
            pltpu.VMEM((2 * rows, wide), BF16),
            pltpu.VMEM((2 * rows, wide), BF16),
            pltpu.VMEM((4 * count, count), F32),
            pltpu.VMEM((8, count, LANES), F32),
            pltpu.VMEM((8, 8, count), F32),
            pltpu.VMEM((8, 2 * rows), F32),
            pltpu.VMEM((16, 8, 2 * rows), F32),
            pltpu.VMEM((16, LANES), F32),
            pltpu.VMEM((8, 16, LANES), F32),
            pltpu.VMEM((8, 8, count), F32),
            pltpu.VMEM((8, 8, count), F32),
            dma((5, NC)), dma((8, NC)), dma((15,)), dma((15,)), dma((7,)), dma((7,)),
            dma((15,)), dma((15,)), dma((7,)), dma((7,)), dma((8,)), dma((8,)),
        ],
        compiler_params=pltpu.CompilerParams(
            collective_id=0, has_side_effects=True, vmem_limit_bytes=56 * 2**20
        ),
    )(small_emb, cluster_of.reshape(1, rows), big_emb)
    return jnp.maximum(small_max.reshape(rows), -1.0), jnp.maximum(big_max.reshape(count), -1.0)


def solution(mesh):
    return jax.shard_map(
        body,
        mesh=mesh,
        in_specs=(P(("blk", "owner"), None), P(("blk", "owner")), P(("blk", "owner"), None)),
        out_specs=(P(("blk", "owner")), P(("blk", "owner"))),
        check_vma=False,
    )
```

```python
import functools

import jax
import jax.numpy as jnp
from jax import lax
from jax.experimental import pallas as pl
from jax.experimental.pallas import tpu as pltpu
from jax.sharding import PartitionSpec as P

MESH = pl.DeviceIdType.MESH
F32 = jnp.float32
BF16 = jnp.bfloat16
CPO = 16
LANES = 128
CHUNK = 32
NC = 8
KC = 1024

HOMES = ((0, -2), (0, -1), (0, 0), (1, 1), (1, 0), (-1, 0), (1, 2), (2, -2))
E2, E1, E0, O3, O2, O1, O4, E3 = range(8)
AT_ONCE = 3
RELEASE = 4
GATE = 6
SMALL_HOPS = [(dy, dz) for dy in range(4) for dz in range(4) if (dy, dz) != (0, 0)]
NEAR_FIRST = (
    (1, 0), (3, 0), (2, 0), (0, 1), (0, 3), (1, 1), (3, 3), (1, 3), (3, 1),
    (2, 2), (0, 2), (2, 1), (1, 2), (2, 3), (3, 2),
)
X_HOPS = ((0, 1), (1, 0), (3, 1), (1, 1), (3, 0), (2, 0), (2, 1))


def pick(index, table):
    value = jnp.int32(table[0])
    for place, entry in enumerate(table[1:], 1):
        value = jnp.where(index == place, jnp.int32(entry), value)
    return value


def nt_dot(a, b):
    return lax.dot_general(a, b, (((1,), (1,)), ((), ())), preferred_element_type=F32)


def unit(values):
    values = values.astype(F32)
    inverse = lax.rsqrt(jnp.sum(values * values, axis=-1, keepdims=True) + 1e-06)
    return (values * inverse).astype(BF16)


def fold(values):
    rows, cols = values.shape
    return jnp.max(values.reshape(rows // 8, 8, cols), axis=0)


def iota(shape, dim):
    return lax.broadcasted_iota(jnp.int32, shape, dim)


def kernel(
    small_ref, cluster_ref, big_ref, small_out, big_out,
    hold, units, sbuf, rbuf, qbuf, tbuf, acc, rowacc, colacc, vsend, vbuf, wsend, wbuf, retsend, ret,
    big_ssem, big_rsem, yz_ssem, yz_rsem, x_ssem, x_rsem, v_ssem, v_rsem, w_ssem, w_rsem, ret_ssem, ret_rsem, go_sem,
):
    width = small_ref.shape[1]
    wide = width + LANES
    rows = small_ref.shape[0]
    slots = 2 * rows
    b = lax.axis_index("blk")
    o = lax.axis_index("owner")
    z, y = b // 4, b % 4
    x, core = o // 2, o % 2
    sign = 1 - 2 * core
    hub = (y + core) % 2 == 0

    def blk_at(dy, dz):
        return (z + dz + 4) % 4 * 4 + (y + dy + 4) % 4

    def turned(dy, dz):
        return {"blk": blk_at(sign * dy, dz), "owner": o}

    def row_at(dx, dc):
        return (x + dx) % 4 * 2 + (core + dc) % 2

    barrier = pltpu.get_barrier_semaphore()
    for dy, dz in SMALL_HOPS:
        pl.semaphore_signal(barrier, inc=1, device_id={"blk": blk_at(dy, dz), "owner": o}, device_id_type=MESH)
    for dx, dc in X_HOPS:
        pl.semaphore_signal(barrier, inc=1, device_id={"blk": b, "owner": row_at(dx, dc)}, device_id_type=MESH)

    cluster_lanes = jnp.broadcast_to(cluster_ref[...], (rows, rows))
    cluster_rows = jnp.transpose(cluster_lanes.astype(F32)).astype(jnp.int32)
    owner_lanes, owner_rows = cluster_lanes // CPO, cluster_rows // CPO
    earlier = (owner_lanes == owner_rows) & (iota((rows, rows), 0) < iota((rows, rows), 1))
    rank = jnp.sum(jnp.where(earlier, 1.0, 0.0), axis=0, keepdims=True).astype(jnp.int32)
    owner_of_doc = cluster_ref[...] // CPO
    slot_of_doc = owner_of_doc % 8 * 32 + owner_of_doc // 8 * 2 + rank
    place = jnp.where(iota((slots, rows), 0) == slot_of_doc, 1.0, 0.0).astype(BF16)
    label = jnp.where(iota((rows, LANES), 1) == cluster_rows % CPO, 1.0, 0.0).astype(BF16)

    @pl.loop(0, rows // 16)
    def _(step):
        at = pl.ds(pl.multiple_of(step * 16, 16), 16)
        units[at, :] = unit(small_ref[at, :])

    @pl.loop(0, width // 512)
    def _(step):
        at = pl.ds(pl.multiple_of(step * 512, 512), 512)
        sbuf[:, at] = jnp.dot(place, units[:, at], preferred_element_type=F32).astype(BF16)

    sbuf[:, pl.ds(width, LANES)] = jnp.dot(place, label, preferred_element_type=F32).astype(BF16)

    pl.semaphore_wait(barrier, len(SMALL_HOPS) + len(X_HOPS))

    def big_copy(lane, c, slot, to_slot, to):
        at = pl.ds(pl.multiple_of(c * CHUNK, CHUNK), CHUNK)
        return pltpu.make_async_remote_copy(
            src_ref=hold.at[slot, at],
            dst_ref=hold.at[to_slot, at],
            send_sem=big_ssem.at[lane, c],
            recv_sem=big_rsem.at[to_slot, c],
            device_id=turned(*to),
            device_id_type=MESH,
        )

    def own_right(c):
        return big_copy(0, c, E0, E1, (0, 1))

    def e1_right(c):
        return big_copy(1, c, E1, E2, (0, 1))

    def e2_down(c):
        return big_copy(2, c, E2, E3, (-2, 0))

    def o2_left(c):
        return big_copy(3, c, O2, O3, (0, -1))

    def o3_left(c):
        return big_copy(4, c, O3, O4, (0, -1))

    def own_up(c):
        return big_copy(0, c, E0, O1, (1, 0))

    def own_down(c):
        return big_copy(1, c, E0, O2, (-1, 0))

    def arrived(slot, c):
        big_copy(0, c, slot, slot, (0, 1)).wait_recv()

    def send_own(c):
        for part in range(CHUNK // 16):
            at = pl.ds(pl.multiple_of(c * CHUNK + part * 16, 16), 16)
            hold[E0, at, :] = unit(big_ref[at, :])

        @pl.when(hub)
        def _():
            own_right(c).start()

        @pl.when(jnp.logical_not(hub))
        def _():
            own_down(c).start()
            own_up(c).start()

    def x_copy(n):
        dx, dc = X_HOPS[n]
        to = row_at(dx, dc)
        return pltpu.make_async_remote_copy(
            src_ref=sbuf.at[pl.ds(pl.multiple_of(to * 32, 32), 32)],
            dst_ref=rbuf.at[pl.ds(pl.multiple_of(o * 32, 32), 32)],
            send_sem=x_ssem.at[n],
            recv_sem=x_rsem.at[n],
            device_id={"blk": b, "owner": to},
            device_id_type=MESH,
        )

    for n in range(7):
        x_copy(n).start()
    mine = pl.ds(pl.multiple_of(o * 32, 32), 32)
    rbuf[mine, :] = sbuf[mine, :]

    pl.loop(0, NC)(send_own)

    rowacc[...] = jnp.full(rowacc.shape, -1.0, F32)
    colacc[...] = jnp.full(colacc.shape, -1.0, F32)

    def product(m, n, left, right):
        at = (pl.ds(0, m), pl.ds(0, n))
        acc[at] = nt_dot(left(0), right(0))

        @pl.loop(1, width // KC)
        def _(k):
            acc[at] += nt_dot(left(k), right(k))

    def features(k):
        return pl.ds(pl.multiple_of(k * KC, KC), KC)

    def meet(first, count, slot, r, n):
        size = hold.shape[1]
        m = count * size
        product(
            m,
            n,
            lambda k: hold[pl.ds(first, count), :, features(k)].reshape(m, KC),
            lambda k: hold[slot, pl.ds(r, n), features(k)],
        )
        for step in range(count):
            gram = acc[pl.ds(step * size, size), pl.ds(0, n)]
            if first + step == slot:
                gram = jnp.where(iota(gram.shape, 0) == iota(gram.shape, 1) + r, -1.0, gram)
            at = pl.ds(r, n)
            colacc[slot, :, at] = jnp.maximum(colacc[slot, :, at], fold(gram))
            if first + step != slot:
                for part in range(n // LANES):
                    here = gram[:, part * LANES : (part + 1) * LANES]
                    rowacc[first + step] = jnp.maximum(rowacc[first + step], here)

    def on(role, body):
        pl.when(hub if role else jnp.logical_not(hub))(body)

    def yz_copy(n):
        dy, dz = NEAR_FIRST[n]
        to = blk_at(dy, dz)
        return pltpu.make_async_remote_copy(
            src_ref=qbuf.at[pl.ds(pl.multiple_of(to * 16, 16), 16)],
            dst_ref=tbuf.at[pl.ds(pl.multiple_of(b * 16, 16), 16)],
            send_sem=yz_ssem.at[n],
            recv_sem=yz_rsem.at[n],
            device_id={"blk": to, "owner": o},
            device_id_type=MESH,
        )

    def regroup():
        for n in range(7):
            x_copy(n).wait_recv()
        to_row = iota((slots, slots), 0)
        source = to_row % 16 // 2 * 32 + to_row // 16 * 2 + to_row % 2
        move = jnp.where(iota((slots, slots), 1) == source, 1.0, 0.0).astype(BF16)

        @pl.loop(0, width // 512)
        def _(step):
            at = pl.ds(pl.multiple_of(step * 512, 512), 512)
            qbuf[:, at] = jnp.dot(move, rbuf[:, at], preferred_element_type=F32).astype(BF16)

        tail = pl.ds(width, LANES)
        qbuf[:, tail] = jnp.dot(move, rbuf[:, tail], preferred_element_type=F32).astype(BF16)
        for n in range(AT_ONCE):
            yz_copy(n).start()
        here = pl.ds(pl.multiple_of(b * 16, 16), 16)
        tbuf[here, :] = qbuf[here, :]

    def release():
        other = {"blk": b, "owner": row_at(0, 1)}
        pl.semaphore_signal(go_sem, inc=1, device_id=other, device_id_type=MESH)
        for n in range(AT_ONCE, 15):
            yz_copy(n).start()

    def released():
        pl.semaphore_wait(go_sem, 1)
        for n in range(AT_ONCE, 15):
            yz_copy(n).start()

    def v_copy(n):
        to = blk_at(*NEAR_FIRST[n])
        return pltpu.make_async_remote_copy(
            src_ref=vsend, dst_ref=vbuf.at[b], send_sem=v_ssem.at[n], recv_sem=v_rsem.at[n],
            device_id={"blk": to, "owner": o}, device_id_type=MESH,
        )

    def w_copy(n):
        to = row_at(*X_HOPS[n])
        return pltpu.make_async_remote_copy(
            src_ref=wsend, dst_ref=wbuf.at[o], send_sem=w_ssem.at[n], recv_sem=w_rsem.at[n],
            device_id={"blk": b, "owner": to}, device_id_type=MESH,
        )

    def owner_maxima():
        for n in range(15):
            yz_copy(n).wait_recv()
        product(slots, slots, lambda k: tbuf[:, features(k)], lambda k: tbuf[:, features(k)])
        labels = tbuf[:, pl.ds(width, LANES)]
        same = nt_dot(labels, labels) > 0.5
        same = same & (iota((slots, slots), 0) != iota((slots, slots), 1))
        best = jnp.max(jnp.where(same, acc[pl.ds(0, slots), :], -1.0), axis=0, keepdims=True)
        vsend[...] = jnp.broadcast_to(best, vsend.shape)
        for n in range(15):
            v_copy(n).start()
        vbuf[b] = vsend[...]

    def pass_back():
        for n in range(15):
            v_copy(n).wait_recv()
        for group in range(2):
            packed = vbuf[group * 8]
            for other in range(1, 8):
                packed = jnp.where(iota(packed.shape, 0) == other, vbuf[group * 8 + other], packed)
            packed = pltpu.roll(packed, (16 - b) * 16 % slots, 1)
            wsend[pl.ds(group * 8, 8), :] = packed[:, :LANES]
        for n in range(7):
            w_copy(n).start()
        wbuf[o] = wsend[...]

    def small_result():
        for n in range(7):
            w_copy(n).wait_recv()
        table = wbuf[...].reshape(8 * 16, LANES)
        row_of_doc = owner_of_doc % 8 * 16 + owner_of_doc // 8
        chosen = jnp.where(iota((8 * 16, rows), 0) == row_of_doc, 1.0, 0.0)
        found = lax.dot_general(
            table, chosen, (((0,), (0,)), ((), ())), precision=lax.Precision.HIGHEST, preferred_element_type=F32
        )
        found = jnp.where(iota(found.shape, 0) == 2 * o + rank, found, 0.0)
        small_out[...] = jnp.sum(found, axis=0, keepdims=True)

    def first_steps():
        @pl.loop(0, NC)
        def _(c):
            arrived(O2, c)
            o2_left(c).start()

            @pl.when(c >= GATE)
            def _():
                arrived(E1, c - GATE)
                e1_right(c - GATE).start()

        @pl.loop(NC - GATE, NC)
        def _(c):
            arrived(E1, c)
            e1_right(c).start()

    def o3_steps():
        @pl.loop(0, NC)
        def _(c):
            arrived(O3, c)
            o3_left(c).start()

    def second_step(c, then):
        def body():
            arrived(E2, c)
            e2_down(c).start()
            if c == RELEASE:
                release()
            then()

        return body

    def wait_all(slot, start, stop):
        @pl.loop(start, stop)
        def _(c):
            arrived(slot, c)

    def half(slot, part, first, count):
        start = part * NC // 2
        if slot != E2:
            wait_all(slot, start, start + NC // 2)
        meet(first, count, slot, part * 128, 128)

    on(False, lambda: meet(E0, 1, E0, 0, 256))
    on(True, first_steps)
    regroup()
    on(True, o3_steps)
    on(True, lambda: wait_all(O1, 0, NC))
    on(True, second_step(0, lambda: meet(E1, 4, O1, 0, 256)))
    on(True, second_step(1, lambda: meet(E1, 3, O2, 0, 256)))
    on(True, second_step(2, lambda: meet(E1, 2, E0, 0, 256)))
    on(True, second_step(3, lambda: half(E2, 0, E0, 4)))
    on(True, second_step(4, lambda: half(O4, 0, O2, 2)))
    on(True, second_step(5, lambda: None))
    on(True, second_step(6, lambda: half(E3, 0, E1, 3)))
    on(True, second_step(7, lambda: half(E2, 1, E0, 4)))
    on(True, lambda: half(O4, 1, O2, 2))
    on(False, released)
    owner_maxima()

    def finish(slot):
        whole = jnp.maximum(fold(jnp.transpose(rowacc[slot])), colacc[slot])
        return jnp.broadcast_to(jnp.max(whole, axis=0, keepdims=True), whole.shape)

    def home_copy(slot):
        return pltpu.make_async_remote_copy(
            src_ref=retsend.at[slot], dst_ref=ret.at[slot], send_sem=ret_ssem.at[slot], recv_sem=ret_rsem.at[slot],
            device_id=turned(*HOMES[slot]), device_id_type=MESH,
        )

    def send_home(slots_done):
        for slot in slots_done:
            retsend[slot] = finish(slot)
            home_copy(slot).start()

    def big_result(others):
        best = finish(E0)
        for slot in others:
            home_copy(slot).wait_recv()
            best = jnp.maximum(best, ret[slot])
        big_out[...] = best[0:1]

    def last_pairs():
        send_home((O1, O2, O4))
        half(E3, 1, E2, 4)
        meet(E2, 1, E3, 0, 128)
        send_home((E3, E2, E1, O3))

    def end_hub():
        big_result((E1, E2, E3))

        for slot in (E1, E2, E3, O1, O2, O3, O4):
            home_copy(slot).wait_send()

        @pl.loop(0, NC)
        def _(c):
            own_right(c).wait_send()
            e1_right(c).wait_send()
            e2_down(c).wait_send()
            o2_left(c).wait_send()
            o3_left(c).wait_send()

    def last_relay():
        big_result((O1, O2, O3, O4))

        @pl.loop(0, NC)
        def _(c):
            own_up(c).wait_send()
            own_down(c).wait_send()

    on(True, last_pairs)
    pass_back()
    small_result()
    on(True, end_hub)
    on(False, last_relay)
    for n in range(15):
        yz_copy(n).wait_send()
        v_copy(n).wait_send()
    for n in range(7):
        x_copy(n).wait_send()
        w_copy(n).wait_send()


def body(small_emb, cluster_of, big_emb):
    rows, width = small_emb.shape
    count = big_emb.shape[0]
    wide = width + LANES
    dma = pltpu.SemaphoreType.DMA
    small_max, big_max = pl.pallas_call(
        kernel,
        out_shape=(pltpu.VMEM((1, rows), F32), pltpu.VMEM((1, count), F32)),
        in_specs=[pl.BlockSpec(memory_space=pltpu.VMEM)] * 3,
        out_specs=[pl.BlockSpec(memory_space=pltpu.VMEM)] * 2,
        scratch_shapes=[
            pltpu.VMEM((8, count, width), BF16),
            pltpu.VMEM((rows, width), BF16),
            pltpu.VMEM((2 * rows, wide), BF16),
            pltpu.VMEM((2 * rows, wide), BF16),
            pltpu.VMEM((2 * rows, wide), BF16),
            pltpu.VMEM((2 * rows, wide), BF16),
            pltpu.VMEM((4 * count, count), F32),
            pltpu.VMEM((8, count, LANES), F32),
            pltpu.VMEM((8, 8, count), F32),
            pltpu.VMEM((8, 2 * rows), F32),
            pltpu.VMEM((16, 8, 2 * rows), F32),
            pltpu.VMEM((16, LANES), F32),
            pltpu.VMEM((8, 16, LANES), F32),
            pltpu.VMEM((8, 8, count), F32),
            pltpu.VMEM((8, 8, count), F32),
            dma((5, NC)), dma((8, NC)), dma((15,)), dma((15,)), dma((7,)), dma((7,)),
            dma((15,)), dma((15,)), dma((7,)), dma((7,)), dma((8,)), dma((8,)),
            pltpu.SemaphoreType.REGULAR,
        ],
        compiler_params=pltpu.CompilerParams(
            collective_id=0, has_side_effects=True, vmem_limit_bytes=56 * 2**20
        ),
    )(small_emb, cluster_of.reshape(1, rows), big_emb)
    return jnp.maximum(small_max.reshape(rows), -1.0), jnp.maximum(big_max.reshape(count), -1.0)


def solution(mesh):
    return jax.shard_map(
        body,
        mesh=mesh,
        in_specs=(P(("blk", "owner"), None), P(("blk", "owner")), P(("blk", "owner"), None)),
        out_specs=(P(("blk", "owner")), P(("blk", "owner"))),
        check_vma=False,
    )
```

```python
import functools

import jax
import jax.numpy as jnp
from jax import lax
from jax.experimental import pallas as pl
from jax.experimental.pallas import tpu as pltpu
from jax.sharding import PartitionSpec as P

MESH = pl.DeviceIdType.MESH
F32 = jnp.float32
BF16 = jnp.bfloat16
CPO = 16
LANES = 128
CHUNK = 32
NC = 8
KC = 1024

HOMES = ((0, -2), (0, -1), (0, 0), (1, 1), (1, 0), (-1, 0), (1, 2), (2, -2))
E2, E1, E0, O3, O2, O1, O4, E3 = range(8)
AT_ONCE = 9
RELEASE = 5
AHEAD = 2
GATE = 6
SMALL_HOPS = [(dy, dz) for dy in range(4) for dz in range(4) if (dy, dz) != (0, 0)]
NEAR_FIRST = (
    (1, 0), (3, 0), (2, 0), (0, 1), (0, 3), (1, 1), (3, 3), (1, 3), (3, 1),
    (2, 2), (0, 2), (2, 1), (1, 2), (2, 3), (3, 2),
)
X_HOPS = ((0, 1), (1, 0), (3, 1), (1, 1), (3, 0), (2, 0), (2, 1))


def pick(index, table):
    value = jnp.int32(table[0])
    for place, entry in enumerate(table[1:], 1):
        value = jnp.where(index == place, jnp.int32(entry), value)
    return value


def nt_dot(a, b):
    return lax.dot_general(a, b, (((1,), (1,)), ((), ())), preferred_element_type=F32)


def unit(values):
    values = values.astype(F32)
    inverse = lax.rsqrt(jnp.sum(values * values, axis=-1, keepdims=True) + 1e-06)
    return (values * inverse).astype(BF16)


def fold(values):
    rows, cols = values.shape
    return jnp.max(values.reshape(rows // 8, 8, cols), axis=0)


def iota(shape, dim):
    return lax.broadcasted_iota(jnp.int32, shape, dim)


def kernel(
    small_hbm, cluster_ref, big_hbm, small_out, big_out,
    small_ref, big_ref, in_sem,
    hold, units, sbuf, rbuf, qbuf, tbuf, acc, rowacc, colacc, vsend, vbuf, wsend, wbuf, retsend, ret,
    big_ssem, big_rsem, yz_ssem, yz_rsem, x_ssem, x_rsem, v_ssem, v_rsem, w_ssem, w_rsem, ret_ssem, ret_rsem, go_sem,
):
    big_in = pltpu.make_async_copy(big_hbm, big_ref, in_sem.at[0])
    small_in = pltpu.make_async_copy(small_hbm, small_ref, in_sem.at[1])
    big_in.start()
    small_in.start()
    width = small_ref.shape[1]
    wide = width + LANES
    rows = small_ref.shape[0]
    slots = 2 * rows
    b = lax.axis_index("blk")
    o = lax.axis_index("owner")
    z, y = b // 4, b % 4
    x, core = o // 2, o % 2
    sign = 1 - 2 * core
    hub = (y + core) % 2 == 0

    def blk_at(dy, dz):
        return (z + dz + 4) % 4 * 4 + (y + dy + 4) % 4

    def turned(dy, dz):
        return {"blk": blk_at(sign * dy, dz), "owner": o}

    def row_at(dx, dc):
        return (x + dx) % 4 * 2 + (core + dc) % 2

    barrier = pltpu.get_barrier_semaphore()
    for dy, dz in SMALL_HOPS:
        pl.semaphore_signal(barrier, inc=1, device_id={"blk": blk_at(dy, dz), "owner": o}, device_id_type=MESH)
    for dx, dc in X_HOPS:
        pl.semaphore_signal(barrier, inc=1, device_id={"blk": b, "owner": row_at(dx, dc)}, device_id_type=MESH)

    cluster_lanes = jnp.broadcast_to(cluster_ref[...], (rows, rows))
    cluster_rows = jnp.transpose(cluster_lanes.astype(F32)).astype(jnp.int32)
    owner_lanes, owner_rows = cluster_lanes // CPO, cluster_rows // CPO
    earlier = (owner_lanes == owner_rows) & (iota((rows, rows), 0) < iota((rows, rows), 1))
    rank = jnp.sum(jnp.where(earlier, 1.0, 0.0), axis=0, keepdims=True).astype(jnp.int32)
    owner_of_doc = cluster_ref[...] // CPO
    slot_of_doc = owner_of_doc % 8 * 32 + owner_of_doc // 8 * 2 + rank
    place = jnp.where(iota((slots, rows), 0) == slot_of_doc, 1.0, 0.0).astype(BF16)
    label = jnp.where(iota((rows, LANES), 1) == cluster_rows % CPO, 1.0, 0.0).astype(BF16)

    def place_documents():
        @pl.loop(0, rows // 16)
        def _(step):
            at = pl.ds(pl.multiple_of(step * 16, 16), 16)
            units[at, :] = unit(small_ref[at, :])

        @pl.loop(0, width // 512)
        def _(step):
            at = pl.ds(pl.multiple_of(step * 512, 512), 512)
            sbuf[:, at] = jnp.dot(place, units[:, at], preferred_element_type=F32).astype(BF16)

        sbuf[:, pl.ds(width, LANES)] = jnp.dot(place, label, preferred_element_type=F32).astype(BF16)

    def big_copy(lane, c, slot, to_slot, to):
        at = pl.ds(pl.multiple_of(c * CHUNK, CHUNK), CHUNK)
        return pltpu.make_async_remote_copy(
            src_ref=hold.at[slot, at],
            dst_ref=hold.at[to_slot, at],
            send_sem=big_ssem.at[lane, c],
            recv_sem=big_rsem.at[to_slot, c],
            device_id=turned(*to),
            device_id_type=MESH,
        )

    def own_right(c):
        return big_copy(0, c, E0, E1, (0, 1))

    def e1_right(c):
        return big_copy(1, c, E1, E2, (0, 1))

    def e2_down(c):
        return big_copy(2, c, E2, E3, (-2, 0))

    def o2_left(c):
        return big_copy(3, c, O2, O3, (0, -1))

    def o3_left(c):
        return big_copy(4, c, O3, O4, (0, -1))

    def own_up(c):
        return big_copy(0, c, E0, O1, (1, 0))

    def own_down(c):
        return big_copy(1, c, E0, O2, (-1, 0))

    def arrived(slot, c):
        big_copy(0, c, slot, slot, (0, 1)).wait_recv()

    def send_own(c):
        for part in range(CHUNK // 16):
            at = pl.ds(pl.multiple_of(c * CHUNK + part * 16, 16), 16)
            hold[E0, at, :] = unit(big_ref[at, :])

        @pl.when(hub)
        def _():
            own_right(c).start()

        @pl.when(jnp.logical_not(hub))
        def _():
            own_down(c).start()
            own_up(c).start()

    def x_copy(n):
        dx, dc = X_HOPS[n]
        to = row_at(dx, dc)
        return pltpu.make_async_remote_copy(
            src_ref=sbuf.at[pl.ds(pl.multiple_of(to * 32, 32), 32)],
            dst_ref=rbuf.at[pl.ds(pl.multiple_of(o * 32, 32), 32)],
            send_sem=x_ssem.at[n],
            recv_sem=x_rsem.at[n],
            device_id={"blk": b, "owner": to},
            device_id_type=MESH,
        )

    small_in.wait()
    soon = z < 2
    pl.when(soon)(place_documents)
    big_in.wait()
    pl.semaphore_wait(barrier, len(SMALL_HOPS) + len(X_HOPS))
    pl.loop(0, AHEAD)(send_own)
    pl.when(jnp.logical_not(soon))(place_documents)
    for n in range(7):
        x_copy(n).start()
    mine = pl.ds(pl.multiple_of(o * 32, 32), 32)
    rbuf[mine, :] = sbuf[mine, :]
    pl.loop(AHEAD, NC)(send_own)

    rowacc[...] = jnp.full(rowacc.shape, -1.0, F32)
    colacc[...] = jnp.full(colacc.shape, -1.0, F32)

    def product(m, n, left, right):
        at = (pl.ds(0, m), pl.ds(0, n))
        acc[at] = nt_dot(left(0), right(0))

        @pl.loop(1, width // KC)
        def _(k):
            acc[at] += nt_dot(left(k), right(k))

    def features(k):
        return pl.ds(pl.multiple_of(k * KC, KC), KC)

    def meet(first, count, slot, r, n):
        size = hold.shape[1]
        m = count * size
        product(
            m,
            n,
            lambda k: hold[pl.ds(first, count), :, features(k)].reshape(m, KC),
            lambda k: hold[slot, pl.ds(r, n), features(k)],
        )
        for step in range(count):
            gram = acc[pl.ds(step * size, size), pl.ds(0, n)]
            if first + step == slot:
                gram = jnp.where(iota(gram.shape, 0) == iota(gram.shape, 1) + r, -1.0, gram)
            at = pl.ds(r, n)
            colacc[slot, :, at] = jnp.maximum(colacc[slot, :, at], fold(gram))
            if first + step != slot:
                for part in range(n // LANES):
                    here = gram[:, part * LANES : (part + 1) * LANES]
                    rowacc[first + step] = jnp.maximum(rowacc[first + step], here)

    def on(role, body):
        pl.when(hub if role else jnp.logical_not(hub))(body)

    def yz_copy(n):
        dy, dz = NEAR_FIRST[n]
        to = blk_at(dy, dz)
        return pltpu.make_async_remote_copy(
            src_ref=qbuf.at[pl.ds(pl.multiple_of(to * 16, 16), 16)],
            dst_ref=tbuf.at[pl.ds(pl.multiple_of(b * 16, 16), 16)],
            send_sem=yz_ssem.at[n],
            recv_sem=yz_rsem.at[n],
            device_id={"blk": to, "owner": o},
            device_id_type=MESH,
        )

    def regroup():
        for n in range(7):
            x_copy(n).wait_recv()
        to_row = iota((slots, slots), 0)
        source = to_row % 16 // 2 * 32 + to_row // 16 * 2 + to_row % 2
        move = jnp.where(iota((slots, slots), 1) == source, 1.0, 0.0).astype(BF16)

        @pl.loop(0, width // 512)
        def _(step):
            at = pl.ds(pl.multiple_of(step * 512, 512), 512)
            qbuf[:, at] = jnp.dot(move, rbuf[:, at], preferred_element_type=F32).astype(BF16)

        tail = pl.ds(width, LANES)
        qbuf[:, tail] = jnp.dot(move, rbuf[:, tail], preferred_element_type=F32).astype(BF16)
        for n in range(AT_ONCE):
            yz_copy(n).start()
        here = pl.ds(pl.multiple_of(b * 16, 16), 16)
        tbuf[here, :] = qbuf[here, :]

    def release():
        other = {"blk": b, "owner": row_at(0, 1)}
        pl.semaphore_signal(go_sem, inc=1, device_id=other, device_id_type=MESH)
        for n in range(AT_ONCE, 15):
            yz_copy(n).start()

    def released():
        pl.semaphore_wait(go_sem, 1)
        for n in range(AT_ONCE, 15):
            yz_copy(n).start()

    def v_copy(n):
        to = blk_at(*NEAR_FIRST[n])
        return pltpu.make_async_remote_copy(
            src_ref=vsend, dst_ref=vbuf.at[b], send_sem=v_ssem.at[n], recv_sem=v_rsem.at[n],
            device_id={"blk": to, "owner": o}, device_id_type=MESH,
        )

    def w_copy(n):
        to = row_at(*X_HOPS[n])
        return pltpu.make_async_remote_copy(
            src_ref=wsend, dst_ref=wbuf.at[o], send_sem=w_ssem.at[n], recv_sem=w_rsem.at[n],
            device_id={"blk": b, "owner": to}, device_id_type=MESH,
        )

    def owner_maxima():
        for n in range(15):
            yz_copy(n).wait_recv()
        product(slots, slots, lambda k: tbuf[:, features(k)], lambda k: tbuf[:, features(k)])
        labels = tbuf[:, pl.ds(width, LANES)]
        same = nt_dot(labels, labels) > 0.5
        same = same & (iota((slots, slots), 0) != iota((slots, slots), 1))
        best = jnp.max(jnp.where(same, acc[pl.ds(0, slots), :], -1.0), axis=0, keepdims=True)
        vsend[...] = jnp.broadcast_to(best, vsend.shape)
        for n in range(15):
            v_copy(n).start()
        vbuf[b] = vsend[...]

    def pass_back():
        for n in range(15):
            v_copy(n).wait_recv()
        for group in range(2):
            packed = vbuf[group * 8]
            for other in range(1, 8):
                packed = jnp.where(iota(packed.shape, 0) == other, vbuf[group * 8 + other], packed)
            packed = pltpu.roll(packed, (16 - b) * 16 % slots, 1)
            wsend[pl.ds(group * 8, 8), :] = packed[:, :LANES]
        for n in range(7):
            w_copy(n).start()
        wbuf[o] = wsend[...]

    def small_result():
        for n in range(7):
            w_copy(n).wait_recv()
        table = wbuf[...].reshape(8 * 16, LANES)
        row_of_doc = owner_of_doc % 8 * 16 + owner_of_doc // 8
        chosen = jnp.where(iota((8 * 16, rows), 0) == row_of_doc, 1.0, 0.0)
        found = lax.dot_general(
            table, chosen, (((0,), (0,)), ((), ())), precision=lax.Precision.HIGHEST, preferred_element_type=F32
        )
        found = jnp.where(iota(found.shape, 0) == 2 * o + rank, found, 0.0)
        small_out[...] = jnp.sum(found, axis=0, keepdims=True)

    def first_steps():
        @pl.loop(0, NC)
        def _(c):
            arrived(O2, c)
            o2_left(c).start()

            @pl.when(c >= GATE)
            def _():
                arrived(E1, c - GATE)
                e1_right(c - GATE).start()

        @pl.loop(NC - GATE, NC)
        def _(c):
            arrived(E1, c)
            e1_right(c).start()

    def o3_steps(start, stop):
        def body():
            @pl.loop(start, stop)
            def _(c):
                arrived(O3, c)
                o3_left(c).start()

        return body

    def second_step(c, then):
        def body():
            arrived(E2, c)
            e2_down(c).start()
            if c == RELEASE:
                release()
            then()

        return body

    def wait_all(slot, start, stop):
        @pl.loop(start, stop)
        def _(c):
            arrived(slot, c)

    def half(slot, part, first, count):
        start = part * NC // 2
        if slot != E2:
            wait_all(slot, start, start + NC // 2)
        meet(first, count, slot, part * 128, 128)

    on(False, lambda: meet(E0, 1, E0, 0, 256))
    on(True, first_steps)
    on(True, o3_steps(0, 5))
    regroup()
    on(True, o3_steps(5, NC))
    on(True, lambda: wait_all(O1, 0, NC))
    on(True, second_step(0, lambda: meet(E1, 4, O1, 0, 256)))
    on(True, second_step(1, lambda: meet(E1, 3, O2, 0, 256)))
    on(True, second_step(2, lambda: meet(E1, 2, E0, 0, 256)))
    on(True, second_step(3, lambda: half(E2, 0, E0, 4)))
    on(True, second_step(4, lambda: half(O4, 0, O2, 2)))
    on(True, second_step(5, lambda: None))
    on(True, second_step(6, lambda: half(E3, 0, E1, 3)))
    on(True, second_step(7, lambda: half(E2, 1, E0, 4)))
    on(True, lambda: half(O4, 1, O2, 2))
    on(False, released)
    owner_maxima()

    def finish(slot):
        whole = jnp.maximum(fold(jnp.transpose(rowacc[slot])), colacc[slot])
        return jnp.broadcast_to(jnp.max(whole, axis=0, keepdims=True), whole.shape)

    def home_copy(slot):
        return pltpu.make_async_remote_copy(
            src_ref=retsend.at[slot], dst_ref=ret.at[slot], send_sem=ret_ssem.at[slot], recv_sem=ret_rsem.at[slot],
            device_id=turned(*HOMES[slot]), device_id_type=MESH,
        )

    def send_home(slots_done):
        for slot in slots_done:
            retsend[slot] = finish(slot)
            home_copy(slot).start()

    def big_result(others):
        best = finish(E0)
        for slot in others:
            home_copy(slot).wait_recv()
            best = jnp.maximum(best, ret[slot])
        big_out[...] = best[0:1]

    def last_pairs():
        send_home((O1, O2, O4))
        half(E3, 1, E2, 4)
        meet(E2, 1, E3, 0, 128)
        send_home((E3, E2, E1, O3))

    def end_hub():
        big_result((E1, E2, E3))

        for slot in (E1, E2, E3, O1, O2, O3, O4):
            home_copy(slot).wait_send()

        @pl.loop(0, NC)
        def _(c):
            own_right(c).wait_send()
            e1_right(c).wait_send()
            e2_down(c).wait_send()
            o2_left(c).wait_send()
            o3_left(c).wait_send()

    def last_relay():
        big_result((O1, O2, O3, O4))

        @pl.loop(0, NC)
        def _(c):
            own_up(c).wait_send()
            own_down(c).wait_send()

    on(True, last_pairs)
    pass_back()
    small_result()
    on(True, end_hub)
    on(False, last_relay)
    for n in range(15):
        yz_copy(n).wait_send()
        v_copy(n).wait_send()
    for n in range(7):
        x_copy(n).wait_send()
        w_copy(n).wait_send()


def body(small_emb, cluster_of, big_emb):
    rows, width = small_emb.shape
    count = big_emb.shape[0]
    wide = width + LANES
    dma = pltpu.SemaphoreType.DMA
    small_max, big_max = pl.pallas_call(
        kernel,
        out_shape=(pltpu.VMEM((1, rows), F32), pltpu.VMEM((1, count), F32)),
        in_specs=[pl.BlockSpec(memory_space=space) for space in (pl.ANY, pltpu.VMEM, pl.ANY)],
        out_specs=[pl.BlockSpec(memory_space=pltpu.VMEM)] * 2,
        scratch_shapes=[
            pltpu.VMEM((rows, width), BF16),
            pltpu.VMEM((count, width), BF16),
            dma((2,)),
            pltpu.VMEM((8, count, width), BF16),
            pltpu.VMEM((rows, width), BF16),
            pltpu.VMEM((2 * rows, wide), BF16),
            pltpu.VMEM((2 * rows, wide), BF16),
            pltpu.VMEM((2 * rows, wide), BF16),
            pltpu.VMEM((2 * rows, wide), BF16),
            pltpu.VMEM((4 * count, count), F32),
            pltpu.VMEM((8, count, LANES), F32),
            pltpu.VMEM((8, 8, count), F32),
            pltpu.VMEM((8, 2 * rows), F32),
            pltpu.VMEM((16, 8, 2 * rows), F32),
            pltpu.VMEM((16, LANES), F32),
            pltpu.VMEM((8, 16, LANES), F32),
            pltpu.VMEM((8, 8, count), F32),
            pltpu.VMEM((8, 8, count), F32),
            dma((5, NC)), dma((8, NC)), dma((15,)), dma((15,)), dma((7,)), dma((7,)),
            dma((15,)), dma((15,)), dma((7,)), dma((7,)), dma((8,)), dma((8,)),
            pltpu.SemaphoreType.REGULAR,
        ],
        compiler_params=pltpu.CompilerParams(
            collective_id=0, has_side_effects=True, vmem_limit_bytes=56 * 2**20
        ),
    )(small_emb, cluster_of.reshape(1, rows), big_emb)
    return jnp.maximum(small_max.reshape(rows), -1.0), jnp.maximum(big_max.reshape(count), -1.0)


def solution(mesh):
    return jax.shard_map(
        body,
        mesh=mesh,
        in_specs=(P(("blk", "owner"), None), P(("blk", "owner")), P(("blk", "owner"), None)),
        out_specs=(P(("blk", "owner")), P(("blk", "owner"))),
        check_vma=False,
    )
```

```python
import functools

import jax
import jax.numpy as jnp
from jax import lax
from jax.experimental import pallas as pl
from jax.experimental.pallas import tpu as pltpu
from jax.sharding import PartitionSpec as P

MESH = pl.DeviceIdType.MESH
F32 = jnp.float32
BF16 = jnp.bfloat16
CPO = 16
LANES = 128
CHUNK = 32
NC = 8
KC = 1024

HOMES = ((0, -2), (0, -1), (0, 0), (1, 1), (1, 0), (-1, 0), (1, 2), (2, -2))
E2, E1, E0, O3, O2, O1, O4, E3 = range(8)
AT_ONCE = 9
RELEASE = 3
AHEAD = 2
GATE = 6
SMALL_HOPS = [(dy, dz) for dy in range(4) for dz in range(4) if (dy, dz) != (0, 0)]
NEAR_FIRST = (
    (1, 0), (3, 0), (2, 0), (0, 1), (0, 3), (1, 1), (3, 3), (1, 3), (3, 1),
    (2, 2), (0, 2), (2, 1), (1, 2), (2, 3), (3, 2),
)
X_HOPS = ((0, 1), (1, 0), (3, 1), (1, 1), (3, 0), (2, 0), (2, 1))


def pick(index, table):
    value = jnp.int32(table[0])
    for place, entry in enumerate(table[1:], 1):
        value = jnp.where(index == place, jnp.int32(entry), value)
    return value


def nt_dot(a, b):
    return lax.dot_general(a, b, (((1,), (1,)), ((), ())), preferred_element_type=F32)


def unit(values):
    values = values.astype(F32)
    inverse = lax.rsqrt(jnp.sum(values * values, axis=-1, keepdims=True) + 1e-06)
    return (values * inverse).astype(BF16)


def fold(values):
    rows, cols = values.shape
    return jnp.max(values.reshape(rows // 8, 8, cols), axis=0)


def iota(shape, dim):
    return lax.broadcasted_iota(jnp.int32, shape, dim)


def kernel(
    small_hbm, cluster_ref, big_hbm, small_out, big_out,
    small_ref, big_ref, in_sem,
    hold, units, sbuf, rbuf, qbuf, tbuf, acc, rowacc, colacc, vsend, vbuf, wsend, wbuf, retsend, ret,
    big_ssem, big_rsem, yz_ssem, yz_rsem, x_ssem, x_rsem, v_ssem, v_rsem, w_ssem, w_rsem, ret_ssem, ret_rsem, go_sem,
):
    big_in = pltpu.make_async_copy(big_hbm, big_ref, in_sem.at[0])
    small_in = pltpu.make_async_copy(small_hbm, small_ref, in_sem.at[1])
    big_in.start()
    small_in.start()
    width = small_ref.shape[1]
    wide = width + LANES
    rows = small_ref.shape[0]
    slots = 2 * rows
    b = lax.axis_index("blk")
    o = lax.axis_index("owner")
    z, y = b // 4, b % 4
    x, core = o // 2, o % 2
    sign = 1 - 2 * core
    hub = (y + core) % 2 == 0

    def blk_at(dy, dz):
        return (z + dz + 4) % 4 * 4 + (y + dy + 4) % 4

    def turned(dy, dz):
        return {"blk": blk_at(sign * dy, dz), "owner": o}

    def row_at(dx, dc):
        return (x + dx) % 4 * 2 + (core + dc) % 2

    barrier = pltpu.get_barrier_semaphore()
    for dy, dz in SMALL_HOPS:
        pl.semaphore_signal(barrier, inc=1, device_id={"blk": blk_at(dy, dz), "owner": o}, device_id_type=MESH)
    for dx, dc in X_HOPS:
        pl.semaphore_signal(barrier, inc=1, device_id={"blk": b, "owner": row_at(dx, dc)}, device_id_type=MESH)

    cluster_lanes = jnp.broadcast_to(cluster_ref[...], (rows, rows))
    cluster_rows = jnp.transpose(cluster_lanes.astype(F32)).astype(jnp.int32)
    owner_lanes, owner_rows = cluster_lanes // CPO, cluster_rows // CPO
    earlier = (owner_lanes == owner_rows) & (iota((rows, rows), 0) < iota((rows, rows), 1))
    rank = jnp.sum(jnp.where(earlier, 1.0, 0.0), axis=0, keepdims=True).astype(jnp.int32)
    owner_of_doc = cluster_ref[...] // CPO
    slot_of_doc = owner_of_doc % 8 * 32 + owner_of_doc // 8 * 2 + rank
    place = jnp.where(iota((slots, rows), 0) == slot_of_doc, 1.0, 0.0).astype(BF16)
    label = jnp.where(iota((rows, LANES), 1) == cluster_rows % CPO, 1.0, 0.0).astype(BF16)

    def place_documents():
        @pl.loop(0, rows // 16)
        def _(step):
            at = pl.ds(pl.multiple_of(step * 16, 16), 16)
            units[at, :] = unit(small_ref[at, :])

        @pl.loop(0, width // 512)
        def _(step):
            at = pl.ds(pl.multiple_of(step * 512, 512), 512)
            sbuf[:, at] = jnp.dot(place, units[:, at], preferred_element_type=F32).astype(BF16)

        sbuf[:, pl.ds(width, LANES)] = jnp.dot(place, label, preferred_element_type=F32).astype(BF16)

    def big_copy(lane, c, slot, to_slot, to):
        at = pl.ds(pl.multiple_of(c * CHUNK, CHUNK), CHUNK)
        return pltpu.make_async_remote_copy(
            src_ref=hold.at[slot, at],
            dst_ref=hold.at[to_slot, at],
            send_sem=big_ssem.at[lane, c],
            recv_sem=big_rsem.at[to_slot, c],
            device_id=turned(*to),
            device_id_type=MESH,
        )

    def own_right(c):
        return big_copy(0, c, E0, E1, (0, 1))

    def e1_right(c):
        return big_copy(1, c, E1, E2, (0, 1))

    def e2_down(c):
        return big_copy(2, c, E2, E3, (-2, 0))

    def o2_left(c):
        return big_copy(3, c, O2, O3, (0, -1))

    def o3_left(c):
        return big_copy(4, c, O3, O4, (0, -1))

    def own_up(c):
        return big_copy(0, c, E0, O1, (1, 0))

    def own_down(c):
        return big_copy(1, c, E0, O2, (-1, 0))

    def arrived(slot, c):
        big_copy(0, c, slot, slot, (0, 1)).wait_recv()

    def send_own(c):
        for part in range(CHUNK // 16):
            at = pl.ds(pl.multiple_of(c * CHUNK + part * 16, 16), 16)
            hold[E0, at, :] = unit(big_ref[at, :])

        @pl.when(hub)
        def _():
            own_right(c).start()

        @pl.when(jnp.logical_not(hub))
        def _():
            own_down(c).start()
            own_up(c).start()

    def x_copy(n):
        dx, dc = X_HOPS[n]
        to = row_at(dx, dc)
        return pltpu.make_async_remote_copy(
            src_ref=sbuf.at[pl.ds(pl.multiple_of(to * 32, 32), 32)],
            dst_ref=rbuf.at[pl.ds(pl.multiple_of(o * 32, 32), 32)],
            send_sem=x_ssem.at[n],
            recv_sem=x_rsem.at[n],
            device_id={"blk": b, "owner": to},
            device_id_type=MESH,
        )

    small_in.wait()
    soon = z < 2
    pl.when(soon)(place_documents)
    big_in.wait()
    pl.semaphore_wait(barrier, len(SMALL_HOPS) + len(X_HOPS))
    pl.loop(0, AHEAD)(send_own)
    pl.when(jnp.logical_not(soon))(place_documents)
    for n in range(7):
        x_copy(n).start()
    mine = pl.ds(pl.multiple_of(o * 32, 32), 32)
    rbuf[mine, :] = sbuf[mine, :]
    pl.loop(AHEAD, NC)(send_own)

    rowacc[...] = jnp.full(rowacc.shape, -1.0, F32)
    colacc[...] = jnp.full(colacc.shape, -1.0, F32)

    def product(m, n, left, right):
        at = (pl.ds(0, m), pl.ds(0, n))
        acc[at] = nt_dot(left(0), right(0))

        @pl.loop(1, width // KC)
        def _(k):
            acc[at] += nt_dot(left(k), right(k))

    def features(k):
        return pl.ds(pl.multiple_of(k * KC, KC), KC)

    def meet(first, count, slot, r, n):
        size = hold.shape[1]
        m = count * size
        product(
            m,
            n,
            lambda k: hold[pl.ds(first, count), :, features(k)].reshape(m, KC),
            lambda k: hold[slot, pl.ds(r, n), features(k)],
        )
        for step in range(count):
            gram = acc[pl.ds(step * size, size), pl.ds(0, n)]
            if first + step == slot:
                gram = jnp.where(iota(gram.shape, 0) == iota(gram.shape, 1) + r, -1.0, gram)
            at = pl.ds(r, n)
            colacc[slot, :, at] = jnp.maximum(colacc[slot, :, at], fold(gram))
            if first + step != slot:
                for part in range(n // LANES):
                    here = gram[:, part * LANES : (part + 1) * LANES]
                    rowacc[first + step] = jnp.maximum(rowacc[first + step], here)

    def on(role, body):
        pl.when(hub if role else jnp.logical_not(hub))(body)

    def yz_copy(n):
        dy, dz = NEAR_FIRST[n]
        to = blk_at(dy, dz)
        return pltpu.make_async_remote_copy(
            src_ref=qbuf.at[pl.ds(pl.multiple_of(to * 16, 16), 16)],
            dst_ref=tbuf.at[pl.ds(pl.multiple_of(b * 16, 16), 16)],
            send_sem=yz_ssem.at[n],
            recv_sem=yz_rsem.at[n],
            device_id={"blk": to, "owner": o},
            device_id_type=MESH,
        )

    def regroup():
        for n in range(7):
            x_copy(n).wait_recv()
        to_row = iota((slots, slots), 0)
        source = to_row % 16 // 2 * 32 + to_row // 16 * 2 + to_row % 2
        move = jnp.where(iota((slots, slots), 1) == source, 1.0, 0.0).astype(BF16)

        @pl.loop(0, width // 512)
        def _(step):
            at = pl.ds(pl.multiple_of(step * 512, 512), 512)
            qbuf[:, at] = jnp.dot(move, rbuf[:, at], preferred_element_type=F32).astype(BF16)

        tail = pl.ds(width, LANES)
        qbuf[:, tail] = jnp.dot(move, rbuf[:, tail], preferred_element_type=F32).astype(BF16)
        for n in range(AT_ONCE):
            yz_copy(n).start()
        here = pl.ds(pl.multiple_of(b * 16, 16), 16)
        tbuf[here, :] = qbuf[here, :]

    def release():
        other = {"blk": b, "owner": row_at(0, 1)}
        pl.semaphore_signal(go_sem, inc=1, device_id=other, device_id_type=MESH)
        for n in range(AT_ONCE, 15):
            yz_copy(n).start()

    def released():
        pl.semaphore_wait(go_sem, 1)
        for n in range(AT_ONCE, 15):
            yz_copy(n).start()

    def v_copy(n):
        to = blk_at(*NEAR_FIRST[n])
        return pltpu.make_async_remote_copy(
            src_ref=vsend, dst_ref=vbuf.at[b], send_sem=v_ssem.at[n], recv_sem=v_rsem.at[n],
            device_id={"blk": to, "owner": o}, device_id_type=MESH,
        )

    def w_copy(n):
        to = row_at(*X_HOPS[n])
        return pltpu.make_async_remote_copy(
            src_ref=wsend, dst_ref=wbuf.at[o], send_sem=w_ssem.at[n], recv_sem=w_rsem.at[n],
            device_id={"blk": b, "owner": to}, device_id_type=MESH,
        )

    def owner_maxima():
        for n in range(15):
            yz_copy(n).wait_recv()
        product(slots, slots, lambda k: tbuf[:, features(k)], lambda k: tbuf[:, features(k)])
        labels = tbuf[:, pl.ds(width, LANES)]
        same = nt_dot(labels, labels) > 0.5
        same = same & (iota((slots, slots), 0) != iota((slots, slots), 1))
        best = jnp.max(jnp.where(same, acc[pl.ds(0, slots), :], -1.0), axis=0, keepdims=True)
        vsend[...] = jnp.broadcast_to(best, vsend.shape)
        for n in range(15):
            v_copy(n).start()
        vbuf[b] = vsend[...]

    def pass_back():
        for n in range(15):
            v_copy(n).wait_recv()
        for group in range(2):
            packed = vbuf[group * 8]
            for other in range(1, 8):
                packed = jnp.where(iota(packed.shape, 0) == other, vbuf[group * 8 + other], packed)
            packed = pltpu.roll(packed, (16 - b) * 16 % slots, 1)
            wsend[pl.ds(group * 8, 8), :] = packed[:, :LANES]
        for n in range(7):
            w_copy(n).start()
        wbuf[o] = wsend[...]

    def small_result():
        for n in range(7):
            w_copy(n).wait_recv()
        table = wbuf[...].reshape(8 * 16, LANES)
        row_of_doc = owner_of_doc % 8 * 16 + owner_of_doc // 8
        chosen = jnp.where(iota((8 * 16, rows), 0) == row_of_doc, 1.0, 0.0)
        found = lax.dot_general(
            table, chosen, (((0,), (0,)), ((), ())), precision=lax.Precision.HIGHEST, preferred_element_type=F32
        )
        found = jnp.where(iota(found.shape, 0) == 2 * o + rank, found, 0.0)
        small_out[...] = jnp.sum(found, axis=0, keepdims=True)

    def first_steps():
        @pl.loop(0, NC)
        def _(c):
            arrived(O2, c)
            o2_left(c).start()

            @pl.when(c >= GATE)
            def _():
                arrived(E1, c - GATE)
                e1_right(c - GATE).start()

        @pl.loop(NC - GATE, NC)
        def _(c):
            arrived(E1, c)
            e1_right(c).start()

    def o3_steps(start, stop):
        def body():
            @pl.loop(start, stop)
            def _(c):
                arrived(O3, c)
                o3_left(c).start()

        return body

    def second_step(c, then):
        def body():
            arrived(E2, c)
            e2_down(c).start()
            if c == RELEASE:
                release()
            then()

        return body

    def wait_all(slot, start, stop):
        @pl.loop(start, stop)
        def _(c):
            arrived(slot, c)

    def half(slot, part, first, count):
        start = part * NC // 2
        if slot != E2:
            wait_all(slot, start, start + NC // 2)
        meet(first, count, slot, part * 128, 128)

    on(False, lambda: meet(E0, 1, E0, 0, 256))
    on(True, first_steps)
    on(True, o3_steps(0, 5))
    regroup()
    on(True, o3_steps(5, NC))
    on(True, lambda: wait_all(O1, 0, NC))
    on(True, second_step(0, lambda: meet(E1, 4, O1, 0, 256)))
    on(True, second_step(1, lambda: meet(E1, 3, O2, 0, 256)))
    on(True, second_step(2, lambda: meet(E1, 2, E0, 0, 256)))
    on(True, second_step(3, lambda: half(E2, 0, E0, 4)))
    on(True, second_step(4, lambda: half(O4, 0, O2, 2)))
    on(True, second_step(5, lambda: None))
    on(True, second_step(6, lambda: half(E3, 0, E1, 3)))
    on(True, second_step(7, lambda: half(E2, 1, E0, 4)))
    on(True, lambda: half(O4, 1, O2, 2))
    on(False, released)
    owner_maxima()

    def finish(slot):
        whole = jnp.maximum(fold(jnp.transpose(rowacc[slot])), colacc[slot])
        return jnp.broadcast_to(jnp.max(whole, axis=0, keepdims=True), whole.shape)

    def home_copy(slot):
        return pltpu.make_async_remote_copy(
            src_ref=retsend.at[slot], dst_ref=ret.at[slot], send_sem=ret_ssem.at[slot], recv_sem=ret_rsem.at[slot],
            device_id=turned(*HOMES[slot]), device_id_type=MESH,
        )

    def send_home(slots_done):
        for slot in slots_done:
            retsend[slot] = finish(slot)
            home_copy(slot).start()

    def big_result(others):
        best = finish(E0)
        for slot in others:
            home_copy(slot).wait_recv()
            best = jnp.maximum(best, ret[slot])
        big_out[...] = best[0:1]

    def last_pairs():
        send_home((O1, O2, O4))
        half(E3, 1, E2, 4)
        meet(E2, 1, E3, 0, 128)
        send_home((E3, E2, E1, O3))

    def end_hub():
        big_result((E1, E2, E3))

        for slot in (E1, E2, E3, O1, O2, O3, O4):
            home_copy(slot).wait_send()

        @pl.loop(0, NC)
        def _(c):
            own_right(c).wait_send()
            e1_right(c).wait_send()
            e2_down(c).wait_send()
            o2_left(c).wait_send()
            o3_left(c).wait_send()

    def last_relay():
        big_result((O1, O2, O3, O4))

        @pl.loop(0, NC)
        def _(c):
            own_up(c).wait_send()
            own_down(c).wait_send()

    on(True, last_pairs)
    pass_back()
    small_result()
    on(True, end_hub)
    on(False, last_relay)
    for n in range(15):
        yz_copy(n).wait_send()
        v_copy(n).wait_send()
    for n in range(7):
        x_copy(n).wait_send()
        w_copy(n).wait_send()


def body(small_emb, cluster_of, big_emb):
    rows, width = small_emb.shape
    count = big_emb.shape[0]
    wide = width + LANES
    dma = pltpu.SemaphoreType.DMA
    small_max, big_max = pl.pallas_call(
        kernel,
        out_shape=(pltpu.VMEM((1, rows), F32), pltpu.VMEM((1, count), F32)),
        in_specs=[pl.BlockSpec(memory_space=space) for space in (pl.ANY, pltpu.VMEM, pl.ANY)],
        out_specs=[pl.BlockSpec(memory_space=pltpu.VMEM)] * 2,
        scratch_shapes=[
            pltpu.VMEM((rows, width), BF16),
            pltpu.VMEM((count, width), BF16),
            dma((2,)),
            pltpu.VMEM((8, count, width), BF16),
            pltpu.VMEM((rows, width), BF16),
            pltpu.VMEM((2 * rows, wide), BF16),
            pltpu.VMEM((2 * rows, wide), BF16),
            pltpu.VMEM((2 * rows, wide), BF16),
            pltpu.VMEM((2 * rows, wide), BF16),
            pltpu.VMEM((4 * count, count), F32),
            pltpu.VMEM((8, count, LANES), F32),
            pltpu.VMEM((8, 8, count), F32),
            pltpu.VMEM((8, 2 * rows), F32),
            pltpu.VMEM((16, 8, 2 * rows), F32),
            pltpu.VMEM((16, LANES), F32),
            pltpu.VMEM((8, 16, LANES), F32),
            pltpu.VMEM((8, 8, count), F32),
            pltpu.VMEM((8, 8, count), F32),
            dma((5, NC)), dma((8, NC)), dma((15,)), dma((15,)), dma((7,)), dma((7,)),
            dma((15,)), dma((15,)), dma((7,)), dma((7,)), dma((8,)), dma((8,)),
            pltpu.SemaphoreType.REGULAR,
        ],
        compiler_params=pltpu.CompilerParams(
            collective_id=0, has_side_effects=True, vmem_limit_bytes=56 * 2**20
        ),
    )(small_emb, cluster_of.reshape(1, rows), big_emb)
    return jnp.maximum(small_max.reshape(rows), -1.0), jnp.maximum(big_max.reshape(count), -1.0)


def solution(mesh):
    return jax.shard_map(
        body,
        mesh=mesh,
        in_specs=(P(("blk", "owner"), None), P(("blk", "owner")), P(("blk", "owner"), None)),
        out_specs=(P(("blk", "owner")), P(("blk", "owner"))),
        check_vma=False,
    )
```
